32 devices in a mesh: grp: 2 (over x), seq: 4 (over y, core), head: 4 (over z).
Axes of the slice: x: 2, y: 2, z: 4, core: 2. Of those that a mesh axis runs over, the one named last changes fastest.
Arguments:
- queries: bfloat16 [256, 4096], P(('grp', 'seq'), 'head'), parts along dimension 0, may hold values from -6 to 6
- root_keys: bfloat16 [8192, 4096], P(('grp', 'seq'), 'head'), parts along dimension 0, may hold values from -6 to 6
- root_values: bfloat16 [8192, 4096], P(('grp', 'seq'), 'head'), parts along dimension 0, may hold values from -6 to 6
- branch_keys: bfloat16 [8192, 4096], P(('grp', 'seq'), 'head'), parts along dimension 0, may hold values from -6 to 6
- branch_values: bfloat16 [8192, 4096], P(('grp', 'seq'), 'head'), parts along dimension 0, may hold values from -6 to 6
- branch_lengths: int32 [8], P(('grp', 'seq')), parts along dimension 0, may hold values from 1 to 1024, 2560 in all
- branch_ids: int32 [256], P('grp'), parts along dimension 0, may hold values from 0 to 3
- slopes: float32 [32], P('head'), may hold values from 0.0001953125 to 0.08
Outputs:
- attended: bfloat16 [256, 4096], P(('grp', 'seq'), 'head'), parts along dimension 0
The draws below stay inside these ranges and needn't reach their ends.
There are 2 independent parts, one for each index of `grp`. The reference program is written for one: setup_inputs(seed, part) draws one part's arguments, and reference() takes and returns one part's arrays. A program takes and returns all parts, laid end to end along the dimension named above; an argument that names none is the same for every part. Nothing has to cross between parts.
Inputs may be any that keep to these rules, and one draw needn't show every extreme that they name: `branch_lengths`: the longest branch holds exactly 1024 live positions; each holds at least one.
All inputs are finite; a program needn't handle non-finite values. No bound on the sum of `branch_lengths` on one device may be relied on, other than what follows from the above.
Results may differ from the reference program's by a relative error of at most 0.0041.
Values may be sent and summed in bfloat16 or wider, within the bound.
No kernel may reach another device: no remote copies, remote signals or barrier semaphores. Data moves between devices by JAX's collectives and lax.ppermute only.
A program may use at most 128 MiB of HBM per device.

```python
import math
import jax
import jax.numpy as jnp
import numpy as np
from jax import lax

HEADS = 32
HEAD_DIM = 128
WIDTH = 4096
QROWS = 128
ROOT_DEV = 1024
ROOT = 4096
BRANCH = 1024
NBR = 4


def draw_queries(key, part):
    base = jnp.clip(jax.random.normal(jax.random.fold_in(key, 1), (QROWS, WIDTH), jnp.float32), -6.0, 6.0)
    return base.astype(jnp.bfloat16)


def draw_root_keys(key, part):
    base = jnp.clip(jax.random.normal(jax.random.fold_in(key, 2), (ROOT, WIDTH), jnp.float32), -6.0, 6.0)
    return base.astype(jnp.bfloat16)


def place_ends(values, key, low, high):
    extent = values.shape
    spot = [jax.random.randint(jax.random.fold_in(key, axis), (), 0, extent[axis]) for axis in range(len(extent))]
    values = values.at[tuple(spot)].set(low)
    longest = extent.index(max(extent))
    spot[longest] = (spot[longest] + 1) % extent[longest]
    return values.at[tuple(spot)].set(high)


def block_scale(rng, shape, cuts, least, largest):
    level = 1.0
    for dim, shards_of in cuts:
        draws = jax.random.uniform(jax.random.fold_in(jax.random.fold_in(rng, 6), dim), (shards_of,), jnp.float32, least / len(cuts), largest / len(cuts))
        level = level * jnp.repeat(jnp.exp(draws), shape[dim] // shards_of).reshape((-1,) + (1,) * (len(shape) - 1 - dim))
    return level


def split_up(count, total, most, lean):
    weights = [(1 << 20) // math.isqrt(rank ** lean) + 1 for rank in range(2, count + 1)]
    rest, counts = total - most - (count - 1), [1] * (count - 1)
    while rest > 0:
        candidates = [i for i in range(count - 1) if counts[i] < most]
        mass, left = sum([weights[i] for i in candidates]), rest
        for i in candidates:
            more = min(most - counts[i], max(1, left * weights[i] // mass), rest)
            counts[i] = counts[i] + more
            rest = rest - more
    return np.array([most] + counts)


def uneven(rng, amount, total, most, lean):
    if amount == 2:
        one = jax.random.randint(rng, (), max(1, total - most), min(most, total - 1) + 1)
        return jnp.stack([one, total - one])
    lengths = jnp.asarray(split_up(amount, total, most, lean), jnp.int32)
    twos = (amount - 1) // 2
    donor, taker = lengths[1:1 + 2 * twos:2], lengths[2:2 + 2 * twos:2]
    margin = jnp.minimum(donor - 1, most - taker)
    passed = jax.random.randint(jax.random.fold_in(rng, 1), (twos,), 0, 1 << 20) % (margin + 1)
    lengths = lengths.at[1:1 + 2 * twos:2].set(donor - passed).at[2:2 + 2 * twos:2].set(taker + passed)
    return lengths[jax.random.permutation(jax.random.fold_in(rng, 2), amount)]


def gaussian(rng, extent, deviation, limit, split=(), held_as=jnp.bfloat16):
    entries = jax.random.normal(rng, extent, jnp.float32) * deviation
    if len(split) > 0:
        entries = block_scale(rng, extent, split, -0.22, 0.18) * entries
    return jnp.clip(entries, min=-limit, max=limit).astype(held_as)


def setup_inputs(seed: int = 0, part: int = 0) -> dict:
    arg_keys = jax.random.split(jax.random.key(seed), 9)
    own_keys = jax.random.split(jax.random.fold_in(arg_keys[8], part), 9)
    return {
        "queries": draw_queries(jax.random.fold_in(jax.random.fold_in(arg_keys[8], part), 71), part),
        "root_keys": draw_root_keys(jax.random.fold_in(jax.random.fold_in(arg_keys[8], part), 71), part),
        "root_values": gaussian(own_keys[2], (ROOT, WIDTH), 1.0, 6.0, ((0, 4), (1, 4))),
        "branch_keys": gaussian(own_keys[3], (NBR * BRANCH, WIDTH), 1.0, 6.0, ((0, 4), (1, 4))),
        "branch_values": gaussian(own_keys[4], (NBR * BRANCH, WIDTH), 1.0, 6.0, ((0, 4), (1, 4))),
        "branch_lengths": uneven(own_keys[5], NBR, NBR * BRANCH * 5 // 8, BRANCH, 2).astype(jnp.int32),
        "branch_ids": place_ends(jax.random.randint(own_keys[6], (QROWS,), 0, NBR), jax.random.fold_in(own_keys[6], 1), 0, NBR - 1).astype(jnp.int32),
        "slopes": jnp.clip(jnp.exp(math.log(0.08) - 6.015181 * jax.random.uniform(arg_keys[7], (HEADS,), jnp.float32) ** block_scale(arg_keys[7], (HEADS,), ((0, 4),), -0.2, 0.2)), 0.0001953125, 0.08),
    }


def reference(queries, root_keys, root_values, branch_keys, branch_values, branch_lengths, branch_ids, slopes):
    scale = 1.0 / (HEAD_DIM ** 0.5)
    query_heads = jnp.transpose(queries.reshape(QROWS, HEADS, HEAD_DIM), (1, 0, 2))
    rkey_heads = jnp.transpose(root_keys.reshape(ROOT, HEADS, HEAD_DIM), (1, 0, 2))
    rval_heads = jnp.transpose(root_values.reshape(ROOT, HEADS, HEAD_DIM), (1, 0, 2))
    bkey_heads = jnp.transpose(branch_keys.reshape(NBR * BRANCH, HEADS, HEAD_DIM), (1, 0, 2))
    bval_heads = jnp.transpose(branch_values.reshape(NBR * BRANCH, HEADS, HEAD_DIM), (1, 0, 2))
    root_pos = jnp.arange(ROOT).astype(jnp.float32) - (ROOT + BRANCH)
    slot = jnp.arange(NBR * BRANCH)
    owner = (slot // BRANCH).astype(jnp.int32)
    offset = slot % BRANCH
    live = offset < branch_lengths[owner]
    match = (branch_ids[:, None] == owner[None, :]) & live[None, :]
    branch_pos = offset.astype(jnp.float32) - BRANCH
    dims = (((1,), (1,)), ((), ()))

    def one_head(items):
        query, rkey, rval, bkey, bval, slope = items
        scores = lax.dot_general(query, rkey, dims, preferred_element_type=jnp.float32) * scale + slope * root_pos[None, :]
        scores = scores.reshape(QROWS, NBR, ROOT_DEV)
        top_root = jnp.max(scores, axis=2)
        weights = jnp.exp(scores - top_root[:, :, None])
        total_root = jnp.sum(weights, axis=2)
        rounded = lax.optimization_barrier(weights.astype(jnp.bfloat16)).astype(jnp.float32)
        values = rval.astype(jnp.float32).reshape(NBR, ROOT_DEV, HEAD_DIM)
        out_root = jnp.einsum('qjk,jkd->qjd', rounded, values)
        bscores = lax.dot_general(query, bkey, dims, preferred_element_type=jnp.float32) * scale + slope * branch_pos[None, :]
        top_branch = jnp.max(jnp.where(match, bscores, -jnp.inf), axis=1)
        bweights = jnp.where(match, jnp.exp(bscores - top_branch[:, None]), 0.0)
        total_branch = jnp.sum(bweights, axis=1)
        out_branch = jnp.dot(bweights.astype(jnp.bfloat16), bval, preferred_element_type=jnp.float32)
        top = jnp.maximum(jnp.max(top_root, axis=1), top_branch)
        factor_root = jnp.exp(top_root - top[:, None])
        factor_branch = jnp.exp(top_branch - top)
        numer = jnp.sum(factor_root[:, :, None] * out_root, axis=1) + factor_branch[:, None] * out_branch
        denom = jnp.sum(factor_root * total_root, axis=1) + factor_branch * total_branch
        return numer / denom[:, None]

    result = lax.map(one_head, (query_heads, rkey_heads, rval_heads, bkey_heads, bval_heads, slopes))
    return jnp.transpose(result, (1, 0, 2)).reshape(QROWS, WIDTH).astype(jnp.bfloat16)
```

```python
import functools
import math

import jax
import jax.numpy as jnp
from jax import lax
from jax.experimental import pallas as pl
from jax.experimental.pallas import tpu as pltpu
from jax.sharding import PartitionSpec as P

LOG2E = math.log2(math.e)
DEAD = -1e30
LANES = 128
HBM = pl.BlockSpec(memory_space=pltpu.HBM)
SMEM = pl.BlockSpec(memory_space=pltpu.SMEM)
VMEM = pl.BlockSpec(memory_space=pltpu.VMEM)


def load_kernel(chunks, root_k, root_v, branch_k, branch_v, root_kt, root_vv, branch_kt, branch_vv, held, sems):
    rows = root_k.shape[0] // chunks
    copies = []
    for i, (src, slot) in enumerate(((root_k, 0), (branch_k, 1))):
        for j in range(chunks):
            part = pl.ds(j * rows, rows)
            copies.append(pltpu.make_async_copy(src.at[part], held.at[slot, part], sems.at[i * chunks + j]))
    values = [
        pltpu.make_async_copy(root_v, root_vv, sems.at[2 * chunks]),
        pltpu.make_async_copy(branch_v, branch_vv, sems.at[2 * chunks + 1]),
    ]
    for copy in copies + values:
        copy.start()
    for slot, out in ((0, root_kt), (1, branch_kt)):
        for j in range(chunks):
            copies[slot * chunks + j].wait()
            part = slice(j * rows, (j + 1) * rows)
            for col in range(0, root_k.shape[1], LANES):
                out[col : col + LANES, part] = held[slot, part, col : col + LANES].T
    for copy in values:
        copy.wait()


def load(root_k, root_v, branch_k, branch_v):
    chunks = 4
    keys, width = root_k.shape
    return pl.pallas_call(
        functools.partial(load_kernel, chunks),
        out_shape=(
            jax.ShapeDtypeStruct((width, keys), root_k.dtype),
            jax.ShapeDtypeStruct((keys, width), root_k.dtype),
            jax.ShapeDtypeStruct((width, keys), root_k.dtype),
            jax.ShapeDtypeStruct((keys, width), root_k.dtype),
        ),
        in_specs=[HBM] * 4,
        out_specs=[VMEM] * 4,
        scratch_shapes=[
            pltpu.VMEM((2, keys, width), root_k.dtype),
            pltpu.SemaphoreType.DMA((2 * chunks + 2,)),
        ],
        compiler_params=pltpu.CompilerParams(vmem_limit_bytes=44 << 20),
        cost_estimate=pl.CostEstimate(flops=0, bytes_accessed=8 * keys * width, transcendentals=0),
        name="load",
    )(root_k, root_v, branch_k, branch_v)


def attend_kernel(shifts, wide, slopes, lengths, ids, *refs):
    blocks, (root_kt, root_v, branch_kt, branch_v) = refs[: len(shifts)], refs[len(shifts) : len(shifts) + 4]
    outs = refs[len(shifts) + 4 + wide :]
    me = lax.axis_index("seq")
    count = lax.axis_size("seq")
    heads = slopes.shape[0]
    rows = blocks[0].shape[0]
    width = blocks[0].shape[1]
    size = width // heads
    keys = root_kt.shape[1]
    every = rows * len(shifts)
    factor = LOG2E / math.sqrt(size)
    spot = lax.broadcasted_iota(jnp.int32, (1, keys), 1)
    place = spot.astype(jnp.float32)
    root_pos = (place + (me * keys).astype(jnp.float32)) - float(keys * count + branch_v.shape[0])
    branch_pos = place - float(branch_v.shape[0])
    dead = jnp.where(spot < lengths[0], 0.0, DEAD)
    all_ids = jnp.broadcast_to(ids[...].reshape(1, -1), (rows, ids.shape[0]))
    lane = lax.broadcasted_iota(jnp.int32, all_ids.shape, 1)
    sub = lax.broadcasted_iota(jnp.int32, all_ids.shape, 0)
    own = []
    for shift in shifts:
        at = lane == sub + jnp.bitwise_xor(me, shift) * rows
        own.append(jnp.sum(jnp.where(at & (all_ids == me), 1.0, 0.0), axis=1, keepdims=True))
    own = jnp.concatenate(own, axis=0) > 0.5
    own = jnp.concatenate([own, own], axis=0)
    zero = jnp.zeros((every, size), blocks[0].dtype)
    units = [(head, part) for head in range(0, heads, 2) for part in (0, 1)]

    def scores(unit):
        head, part = unit
        first = jnp.concatenate([b[:, head * size : (head + 1) * size] for b in blocks], axis=0)
        second = jnp.concatenate([b[:, (head + 1) * size : (head + 2) * size] for b in blocks], axis=0)
        left = jnp.concatenate(
            [jnp.concatenate([first, zero], axis=1), jnp.concatenate([zero, second], axis=1)], axis=0
        )
        key = (root_kt, branch_kt)[part][head * size : (head + 2) * size, :]
        return jnp.dot(left, key, preferred_element_type=jnp.float32)

    ahead = scores(units[0])
    column = lax.broadcasted_iota(jnp.int32, (every, LANES), 1)
    level = jnp.zeros((every, LANES), jnp.float32)
    seen = []
    for i, (head, part) in enumerate(units):
        raw = ahead
        if i + 1 < len(units):
            ahead = scores(units[i + 1])
        shaped = []
        for k in range(2):
            slope = slopes[head + k] * LOG2E
            bias = slope * root_pos if part == 0 else slope * branch_pos + dead
            shaped.append(raw[k * every : (k + 1) * every] * factor + bias)
        shaped = jnp.concatenate(shaped, axis=0)
        top = jnp.max(shaped, axis=1, keepdims=True)
        weight = jnp.exp2(shaped - top)
        total = jnp.sum(weight, axis=1, keepdims=True)
        value = (root_v, branch_v)[part][:, head * size : (head + 2) * size]
        mixed = jnp.dot(weight.astype(value.dtype), value, preferred_element_type=jnp.float32)
        mixed = jnp.concatenate([mixed[:every, :size], mixed[every:, size:]], axis=0)
        seen.append((top, total, mixed))
        if part == 1:
            (top_r, total_r, mixed_r), (top_b, total_b, mixed_b) = seen
            seen = []
            top = jnp.maximum(top_r, jnp.where(own, top_b, DEAD))
            scale_r = jnp.exp2(top_r - top)
            scale_b = jnp.where(own, jnp.exp2(top_b - top), 0.0)
            total = scale_r * total_r + scale_b * total_b
            mixed = (scale_r * mixed_r + scale_b * mixed_b) / total
            log = top + jnp.log2(total)
            for k in range(2):
                cols = slice((head + k) * size, (head + k + 1) * size)
                half = log[k * every : (k + 1) * every]
                level = jnp.where(lax.rem(column, heads) == head + k, half, level)
                for j, out in enumerate(outs):
                    at = slice(k * every + j * rows, k * every + (j + 1) * rows)
                    out[:, cols] = mixed[at].astype(out.dtype)
    if True:
        high = level.astype(jnp.bfloat16).astype(jnp.float32)
        middle = (level - high).astype(jnp.bfloat16).astype(jnp.float32)
        low = level - high - middle
        coded = jnp.where(column < heads, high, jnp.where(column < 2 * heads, middle, low))
    else:
        coded = level
    coded = jnp.where(column < 3 * heads, coded, 0.0)
    for j, out in enumerate(outs):
        out[:, width:] = coded[j * rows : (j + 1) * rows].astype(out.dtype)


def attend(shifts, blocks, slopes, lengths, ids, caches, after):
    rows, width = blocks[0].shape
    keys = caches[0].shape[1]
    return pl.pallas_call(
        functools.partial(attend_kernel, tuple(shifts), len(after)),
        out_shape=tuple(jax.ShapeDtypeStruct((rows, width + LANES), jnp.bfloat16) for _ in shifts),
        in_specs=[SMEM, SMEM, VMEM] + [VMEM] * len(blocks) + [VMEM] * 4 + [pl.BlockSpec(memory_space=pl.ANY)] * len(after),
        out_specs=[VMEM] * len(shifts),
        compiler_params=pltpu.CompilerParams(vmem_limit_bytes=24 << 20),
        cost_estimate=pl.CostEstimate(
            flops=8 * rows * len(shifts) * width * keys,
            bytes_accessed=8 * keys * width,
            transcendentals=2 * rows * len(shifts) * keys * slopes.shape[0],
        ),
        name="attend",
    )(slopes, lengths, ids, *blocks, *caches, *after)


def spread_logs(heads, size, coded):
    row = lax.broadcasted_iota(jnp.int32, (LANES, heads * size), 0)
    col = lax.broadcasted_iota(jnp.int32, (LANES, heads * size), 1)
    spread = jnp.where((lax.rem(row, heads) == col // size) & (row < 3 * heads), 1.0, 0.0).astype(coded.dtype)
    return jnp.dot(coded, spread, preferred_element_type=jnp.float32)


def merge_kernel(heads, last, *refs):
    parts, outs = (refs[:-1], refs[-1:]) if last else (refs[:-2], refs[-2:])
    width = outs[0].shape[1]
    logs, values = [], []
    for i, ref in enumerate(parts):
        if last and i == 0:
            continue
        if last and i == 1:
            logs.append(ref[...])
            values.append(parts[0][...])
        else:
            logs.append(spread_logs(heads, width // heads, ref[:, width:]))
            values.append(ref[:, :width].astype(jnp.float32))
    top = functools.reduce(jnp.maximum, logs)
    scales = [jnp.exp2(log - top) for log in logs]
    total = functools.reduce(jnp.add, scales)
    mixed = functools.reduce(jnp.add, [scale * value for scale, value in zip(scales, values)]) / total
    if last:
        outs[0][...] = mixed.astype(outs[0].dtype)
    else:
        outs[0][...] = mixed
        outs[1][...] = top + jnp.log2(total)


def merge(heads, parts, rows, width, last):
    whole = jax.ShapeDtypeStruct((rows, width), jnp.float32)
    return pl.pallas_call(
        functools.partial(merge_kernel, heads, last),
        out_shape=jax.ShapeDtypeStruct((rows, width), jnp.bfloat16) if last else (whole, whole),
        in_specs=[VMEM] * len(parts),
        out_specs=VMEM if last else (VMEM, VMEM),
        compiler_params=pltpu.CompilerParams(vmem_limit_bytes=8 << 20),
        cost_estimate=pl.CostEstimate(flops=0, bytes_accessed=4 << 20, transcendentals=0),
        name="merge",
    )(*parts)


def shards(queries, root_keys, root_values, branch_keys, branch_values, branch_lengths, branch_ids, slopes):
    count = lax.axis_size("seq")
    rows, width = queries.shape

    def swap(array, shift):
        return lax.ppermute(array, "seq", [(i, i ^ shift) for i in range(count)])

    near, far = (0, 1), tuple(range(2, count))
    blocks = {0: queries}
    for shift in range(2, count, 2):
        blocks[shift] = swap(queries, shift)
    blocks[1] = swap(queries, 1)
    for shift in range(2, count, 2):
        blocks[shift + 1] = swap(blocks[shift], 1)
    caches = load(root_keys, root_values, branch_keys, branch_values)
    sent = attend(far, [blocks[s] for s in far], slopes, branch_lengths, branch_ids, caches, ())
    got = [swap(array, shift) for array, shift in zip(sent, far)]
    kept, passed = attend(near, [blocks[s] for s in near], slopes, branch_lengths, branch_ids, caches, sent[:1])
    mixed, logs = merge(slopes.shape[0], got, rows, width, False)
    return merge(slopes.shape[0], [mixed, logs, kept, swap(passed, 1)], rows, width, True)


def solution(mesh):
    in_specs = (
        P(("grp", "seq"), "head"),
        P(("grp", "seq"), "head"),
        P(("grp", "seq"), "head"),
        P(("grp", "seq"), "head"),
        P(("grp", "seq"), "head"),
        P(("grp", "seq")),
        P("grp"),
        P("head"),
    )
    out_specs = P(("grp", "seq"), "head")
    return jax.shard_map(shards, mesh=mesh, in_specs=in_specs, out_specs=out_specs, check_vma=False)
```

```python
import functools
import math

import jax
import jax.numpy as jnp
from jax import lax
from jax.experimental import pallas as pl
from jax.experimental.pallas import tpu as pltpu
from jax.sharding import PartitionSpec as P

LOG2E = math.log2(math.e)
DEAD = -1e30
LANES = 128
HBM = pl.BlockSpec(memory_space=pltpu.HBM)
SMEM = pl.BlockSpec(memory_space=pltpu.SMEM)
VMEM = pl.BlockSpec(memory_space=pltpu.VMEM)


def load_kernel(chunks, root_k, root_v, branch_k, branch_v, root_kt, root_vv, branch_kt, branch_vv, held, sems):
    rows = root_k.shape[0] // chunks
    copies = []
    for i, (src, slot) in enumerate(((root_k, 0), (branch_k, 1))):
        for j in range(chunks):
            part = pl.ds(j * rows, rows)
            copies.append(pltpu.make_async_copy(src.at[part], held.at[slot, part], sems.at[i * chunks + j]))
    values = [
        pltpu.make_async_copy(root_v, root_vv, sems.at[2 * chunks]),
        pltpu.make_async_copy(branch_v, branch_vv, sems.at[2 * chunks + 1]),
    ]
    for copy in copies + values:
        copy.start()
    for slot, out in ((0, root_kt), (1, branch_kt)):
        for j in range(chunks):
            copies[slot * chunks + j].wait()
            part = slice(j * rows, (j + 1) * rows)
            for col in range(0, root_k.shape[1], LANES):
                out[col : col + LANES, part] = held[slot, part, col : col + LANES].T
    for copy in values:
        copy.wait()


def load(root_k, root_v, branch_k, branch_v):
    chunks = 4
    keys, width = root_k.shape
    return pl.pallas_call(
        functools.partial(load_kernel, chunks),
        out_shape=(
            jax.ShapeDtypeStruct((width, keys), root_k.dtype),
            jax.ShapeDtypeStruct((keys, width), root_k.dtype),
            jax.ShapeDtypeStruct((width, keys), root_k.dtype),
            jax.ShapeDtypeStruct((keys, width), root_k.dtype),
        ),
        in_specs=[HBM] * 4,
        out_specs=[VMEM] * 4,
        scratch_shapes=[
            pltpu.VMEM((2, keys, width), root_k.dtype),
            pltpu.SemaphoreType.DMA((2 * chunks + 2,)),
        ],
        compiler_params=pltpu.CompilerParams(vmem_limit_bytes=44 << 20),
        cost_estimate=pl.CostEstimate(flops=0, bytes_accessed=8 * keys * width, transcendentals=0),
        name="load",
    )(root_k, root_v, branch_k, branch_v)


def column(vector, rows, start):
    wide = jnp.broadcast_to(vector.reshape(1, -1), (rows, vector.shape[0]))
    lane = lax.broadcasted_iota(jnp.int32, wide.shape, 1)
    sub = lax.broadcasted_iota(jnp.int32, wide.shape, 0)
    return jnp.sum(jnp.where(lane == sub + start, wide, jnp.zeros_like(wide)), axis=1, keepdims=True)


def tables_kernel(rows, slopes, lengths, ids, after, bias, mine):
    me = lax.axis_index("seq")
    count = lax.axis_size("seq")
    heads = slopes.shape[0]
    keys = bias.shape[1]
    slope = column(slopes[...], heads, 0) * LOG2E
    spot = lax.broadcasted_iota(jnp.int32, (1, keys), 1)
    place = spot.astype(jnp.float32)
    bias[:heads] = slope * (place + (me * keys - keys * (count + 1)).astype(jnp.float32))
    dead = jnp.where(spot < lengths[...].reshape(1, 1), 0.0, DEAD)
    bias[heads:] = slope * (place - float(keys)) + dead
    mark = jnp.where(ids[...] == me, 1.0, 0.0)
    for shift in range(count):
        at = column(mark, rows, jnp.bitwise_xor(me, shift) * rows)
        mine[shift * rows : (shift + 1) * rows, :] = jnp.broadcast_to(at, (rows, LANES))


def tables(slopes, lengths, ids, rows, keys, after):
    return pl.pallas_call(
        functools.partial(tables_kernel, rows),
        out_shape=(
            jax.ShapeDtypeStruct((2 * slopes.shape[0], keys), jnp.float32),
            jax.ShapeDtypeStruct((ids.shape[0], LANES), jnp.float32),
        ),
        in_specs=[VMEM] * 3 + [pl.BlockSpec(memory_space=pl.ANY)],
        out_specs=[VMEM] * 2,
        compiler_params=pltpu.CompilerParams(vmem_limit_bytes=8 << 20),
        name="tables",
    )(slopes, lengths, ids, after)


def attend_kernel(shifts, heads, skipped, *refs):
    blocks, caches = refs[: len(shifts)], refs[len(shifts) : len(shifts) + 6]
    root_kt, root_v, branch_kt, branch_v, bias, mine = caches
    outs = refs[len(shifts) + 6 + skipped :]
    rows, width = blocks[0].shape
    size = width // heads
    every = rows * len(shifts)
    factor = LOG2E / math.sqrt(size)
    own = jnp.concatenate([mine[shift * rows : (shift + 1) * rows, :1] for shift in shifts] * 2, axis=0) > 0.5
    zero = jnp.zeros((every, size), blocks[0].dtype)
    units = [(head, part) for head in range(0, heads, 2) for part in (0, 1)]

    def scores(unit):
        head, part = unit
        first = jnp.concatenate([b[:, head * size : (head + 1) * size] for b in blocks], axis=0)
        second = jnp.concatenate([b[:, (head + 1) * size : (head + 2) * size] for b in blocks], axis=0)
        left = jnp.concatenate(
            [jnp.concatenate([first, zero], axis=1), jnp.concatenate([zero, second], axis=1)], axis=0
        )
        key = (root_kt, branch_kt)[part][head * size : (head + 2) * size, :]
        return jnp.dot(left, key, preferred_element_type=jnp.float32)

    ahead = scores(units[0])
    lane = lax.broadcasted_iota(jnp.int32, (every, LANES), 1)
    level = jnp.zeros((every, LANES), jnp.float32)
    seen = []
    for i, (head, part) in enumerate(units):
        raw = ahead
        if i + 1 < len(units):
            ahead = scores(units[i + 1])
        shaped = []
        for k in range(2):
            row = part * heads + head + k
            shaped.append(raw[k * every : (k + 1) * every] * factor + bias[row : row + 1, :])
        shaped = jnp.concatenate(shaped, axis=0)
        top = jnp.max(shaped, axis=1, keepdims=True)
        weight = jnp.exp2(shaped - top)
        total = jnp.sum(weight, axis=1, keepdims=True)
        value = (root_v, branch_v)[part][:, head * size : (head + 2) * size]
        mixed = jnp.dot(weight.astype(value.dtype), value, preferred_element_type=jnp.float32)
        mixed = jnp.concatenate([mixed[:every, :size], mixed[every:, size:]], axis=0)
        seen.append((top, total, mixed))
        if part == 1:
            (top_r, total_r, mixed_r), (top_b, total_b, mixed_b) = seen
            seen = []
            top = jnp.maximum(top_r, jnp.where(own, top_b, DEAD))
            scale_r = jnp.exp2(top_r - top)
            scale_b = jnp.where(own, jnp.exp2(top_b - top), 0.0)
            total = scale_r * total_r + scale_b * total_b
            inverse = 1.0 / total
            mixed = (scale_r * inverse) * mixed_r + (scale_b * inverse) * mixed_b
            log = top + jnp.log2(total)
            for k in range(2):
                cols = slice((head + k) * size, (head + k + 1) * size)
                half = log[k * every : (k + 1) * every]
                level = jnp.where(lax.rem(lane, heads) == head + k, half, level)
                for j, out in enumerate(outs):
                    at = slice(k * every + j * rows, k * every + (j + 1) * rows)
                    out[:, cols] = mixed[at].astype(out.dtype)
    high = level.astype(jnp.bfloat16).astype(jnp.float32)
    middle = (level - high).astype(jnp.bfloat16).astype(jnp.float32)
    low = level - high - middle
    coded = jnp.where(lane < heads, high, jnp.where(lane < 2 * heads, middle, low))
    coded = jnp.where(lane < 3 * heads, coded, 0.0)
    for j, out in enumerate(outs):
        out[:, width:] = coded[j * rows : (j + 1) * rows].astype(out.dtype)


def attend(shifts, blocks, heads, caches, after):
    rows, width = blocks[0].shape
    keys = caches[0].shape[1]
    return pl.pallas_call(
        functools.partial(attend_kernel, tuple(shifts), heads, len(after)),
        out_shape=tuple(jax.ShapeDtypeStruct((rows, width + LANES), jnp.bfloat16) for _ in shifts),
        in_specs=[VMEM] * (len(blocks) + len(caches)) + [pl.BlockSpec(memory_space=pl.ANY)] * len(after),
        out_specs=[VMEM] * len(shifts),
        compiler_params=pltpu.CompilerParams(vmem_limit_bytes=24 << 20),
        cost_estimate=pl.CostEstimate(
            flops=8 * rows * len(shifts) * width * keys,
            bytes_accessed=8 * keys * width,
            transcendentals=2 * rows * len(shifts) * keys * heads,
        ),
        name="attend",
    )(*blocks, *caches, *after)


def spread_logs(heads, size, coded):
    row = lax.broadcasted_iota(jnp.int32, (LANES, heads * size), 0)
    col = lax.broadcasted_iota(jnp.int32, (LANES, heads * size), 1)
    spread = jnp.where((lax.rem(row, heads) == col // size) & (row < 3 * heads), 1.0, 0.0).astype(coded.dtype)
    return jnp.dot(coded, spread, preferred_element_type=jnp.float32)


def merge_kernel(heads, last, *refs):
    parts, outs = (refs[:-1], refs[-1:]) if last else (refs[:-2], refs[-2:])
    width = outs[0].shape[1]
    logs, values = [], []
    for i, ref in enumerate(parts):
        if last and i == 0:
            continue
        if last and i == 1:
            logs.append(ref[...])
            values.append(parts[0][...])
        else:
            logs.append(spread_logs(heads, width // heads, ref[:, width:]))
            values.append(ref[:, :width].astype(jnp.float32))
    top = functools.reduce(jnp.maximum, logs)
    scales = [jnp.exp2(log - top) for log in logs]
    total = functools.reduce(jnp.add, scales)
    mixed = functools.reduce(jnp.add, [scale * value for scale, value in zip(scales, values)]) / total
    if last:
        outs[0][...] = mixed.astype(outs[0].dtype)
    else:
        outs[0][...] = mixed
        outs[1][...] = top + jnp.log2(total)


def merge(heads, parts, rows, width, last):
    whole = jax.ShapeDtypeStruct((rows, width), jnp.float32)
    return pl.pallas_call(
        functools.partial(merge_kernel, heads, last),
        out_shape=jax.ShapeDtypeStruct((rows, width), jnp.bfloat16) if last else (whole, whole),
        in_specs=[VMEM] * len(parts),
        out_specs=VMEM if last else (VMEM, VMEM),
        compiler_params=pltpu.CompilerParams(vmem_limit_bytes=8 << 20),
        cost_estimate=pl.CostEstimate(flops=0, bytes_accessed=4 << 20, transcendentals=0),
        name="merge",
    )(*parts)


def shards(queries, root_keys, root_values, branch_keys, branch_values, branch_lengths, branch_ids, slopes):
    count = lax.axis_size("seq")
    rows, width = queries.shape

    def swap(array, shift):
        return lax.ppermute(array, "seq", [(i, i ^ shift) for i in range(count)])

    near, far = (0, 1), tuple(range(2, count))
    blocks = {0: queries} | {shift: swap(queries, shift) for shift in far + near[1:]}
    heads = slopes.shape[0]
    caches = load(root_keys, root_values, branch_keys, branch_values)
    caches += tables(slopes, branch_lengths, branch_ids, rows, root_keys.shape[0], caches[0])
    sent = attend(far, [blocks[s] for s in far], heads, caches, ())
    got = [swap(array, shift) for array, shift in zip(sent, far)]
    kept, passed = attend(near, [blocks[s] for s in near], heads, caches, sent[:1])
    mixed, logs = merge(heads, got, rows, width, False)
    return merge(heads, [mixed, logs, kept, swap(passed, 1)], rows, width, True)


def solution(mesh):
    in_specs = (
        P(("grp", "seq"), "head"),
        P(("grp", "seq"), "head"),
        P(("grp", "seq"), "head"),
        P(("grp", "seq"), "head"),
        P(("grp", "seq"), "head"),
        P(("grp", "seq")),
        P("grp"),
        P("head"),
    )
    out_specs = P(("grp", "seq"), "head")
    return jax.shard_map(shards, mesh=mesh, in_specs=in_specs, out_specs=out_specs, check_vma=False)
```

```python
import functools
import math

import jax
import jax.numpy as jnp
from jax import lax
from jax.experimental import pallas as pl
from jax.experimental.pallas import tpu as pltpu
from jax.sharding import PartitionSpec as P

LOG2E = math.log2(math.e)
DEAD = -1e30
LANES = 128
SUBLANES = 8
ANY = pl.BlockSpec(memory_space=pl.ANY)
HBM = pl.BlockSpec(memory_space=pltpu.HBM)
VMEM = pl.BlockSpec(memory_space=pltpu.VMEM)


def load_kernel(chunks, root_k, root_v, branch_k, branch_v, root_kt, root_vv, branch_kt, branch_vv, held, sems):
    rows = root_k.shape[0] // chunks
    copies = []
    for i, (src, slot) in enumerate(((root_k, 0), (branch_k, 1))):
        for j in range(chunks):
            part = pl.ds(j * rows, rows)
            copies.append(pltpu.make_async_copy(src.at[part], held.at[slot, part], sems.at[i * chunks + j]))
    values = [
        pltpu.make_async_copy(root_v, root_vv, sems.at[2 * chunks]),
        pltpu.make_async_copy(branch_v, branch_vv, sems.at[2 * chunks + 1]),
    ]
    for copy in copies + values:
        copy.start()
    for slot, out in ((0, root_kt), (1, branch_kt)):
        for j in range(chunks):
            copies[slot * chunks + j].wait()
            part = slice(j * rows, (j + 1) * rows)
            for col in range(0, root_k.shape[1], LANES):
                out[col : col + LANES, part] = held[slot, part, col : col + LANES].T
    for copy in values:
        copy.wait()


def load(root_k, root_v, branch_k, branch_v):
    chunks = 4
    keys, width = root_k.shape
    return pl.pallas_call(
        functools.partial(load_kernel, chunks),
        out_shape=(
            jax.ShapeDtypeStruct((width, keys), root_k.dtype),
            jax.ShapeDtypeStruct((keys, width), root_k.dtype),
            jax.ShapeDtypeStruct((width, keys), root_k.dtype),
            jax.ShapeDtypeStruct((keys, width), root_k.dtype),
        ),
        in_specs=[HBM] * 4,
        out_specs=[VMEM] * 4,
        scratch_shapes=[
            pltpu.VMEM((2, keys, width), root_k.dtype),
            pltpu.SemaphoreType.DMA((2 * chunks + 2,)),
        ],
        compiler_params=pltpu.CompilerParams(vmem_limit_bytes=44 << 20),
        cost_estimate=pl.CostEstimate(flops=0, bytes_accessed=8 * keys * width, transcendentals=0),
        name="load",
    )(root_k, root_v, branch_k, branch_v)


def column(vector, rows, start):
    wide = jnp.broadcast_to(vector.reshape(1, -1), (rows, vector.shape[0]))
    lane = lax.broadcasted_iota(jnp.int32, wide.shape, 1)
    sub = lax.broadcasted_iota(jnp.int32, wide.shape, 0)
    return jnp.sum(jnp.where(lane == sub + start, wide, jnp.zeros_like(wide)), axis=1, keepdims=True)


def tables_kernel(rows, slopes, lengths, ids, after, bias, mine):
    me = lax.axis_index("seq")
    count = lax.axis_size("seq")
    heads = slopes.shape[0]
    keys = bias.shape[1]
    slope = column(slopes[...], heads, 0) * LOG2E
    spot = lax.broadcasted_iota(jnp.int32, (1, keys), 1)
    place = spot.astype(jnp.float32)
    bias[:heads] = slope * (place + (me * keys - keys * (count + 1)).astype(jnp.float32))
    dead = jnp.where(spot < lengths[...].reshape(1, 1), 0.0, DEAD)
    bias[heads:] = slope * (place - float(keys)) + dead
    mark = jnp.where(ids[...] == me, 1.0, 0.0)
    for shift in range(count):
        at = column(mark, rows, jnp.bitwise_xor(me, shift) * rows)
        mine[shift * rows : (shift + 1) * rows, :] = jnp.broadcast_to(at, (rows, LANES))


def tables(slopes, lengths, ids, rows, keys, after):
    return pl.pallas_call(
        functools.partial(tables_kernel, rows),
        out_shape=(
            jax.ShapeDtypeStruct((2 * slopes.shape[0], keys), jnp.float32),
            jax.ShapeDtypeStruct((ids.shape[0], LANES), jnp.float32),
        ),
        in_specs=[VMEM] * 3 + [ANY],
        out_specs=[VMEM] * 2,
        compiler_params=pltpu.CompilerParams(vmem_limit_bytes=8 << 20),
        name="tables",
    )(slopes, lengths, ids, after)


def period(rows):
    return LANES // (rows // SUBLANES)


def attend_kernel(shifts, skipped, *refs):
    blocks, caches = refs[: len(shifts)], refs[len(shifts) : len(shifts) + 6]
    root_kt, root_v, branch_kt, branch_v, bias, mine = caches
    outs = refs[len(shifts) + 6 + skipped :]
    rows, width = blocks[0].shape
    heads = bias.shape[0] // 2
    size = width // heads
    every = rows * len(shifts)
    factor = LOG2E / math.sqrt(size)
    own = jnp.concatenate([mine[shift * rows : (shift + 1) * rows, :1] for shift in shifts] * 2, axis=0) > 0.5
    zero = jnp.zeros((every, size), blocks[0].dtype)
    units = [(head, part) for head in range(0, heads, 2) for part in (0, 1)]

    def scores(unit):
        head, part = unit
        first = jnp.concatenate([b[:, head * size : (head + 1) * size] for b in blocks], axis=0)
        second = jnp.concatenate([b[:, (head + 1) * size : (head + 2) * size] for b in blocks], axis=0)
        left = jnp.concatenate(
            [jnp.concatenate([first, zero], axis=1), jnp.concatenate([zero, second], axis=1)], axis=0
        )
        key = (root_kt, branch_kt)[part][head * size : (head + 2) * size, :]
        return jnp.dot(left, key, preferred_element_type=jnp.float32)

    ahead = scores(units[0])
    lane = lax.broadcasted_iota(jnp.int32, (every, LANES), 1)
    place = lax.rem(lane, period(rows))
    level = jnp.zeros((every, LANES), jnp.float32)
    seen = []
    for i, (head, part) in enumerate(units):
        raw = ahead
        if i + 1 < len(units):
            ahead = scores(units[i + 1])
        shaped = []
        for k in range(2):
            row = part * heads + head + k
            shaped.append(raw[k * every : (k + 1) * every] * factor + bias[row : row + 1, :])
        shaped = jnp.concatenate(shaped, axis=0)
        top = jnp.max(shaped, axis=1, keepdims=True)
        weight = jnp.exp2(shaped - top)
        total = jnp.sum(weight, axis=1, keepdims=True)
        value = (root_v, branch_v)[part][:, head * size : (head + 2) * size]
        mixed = jnp.dot(weight.astype(value.dtype), value, preferred_element_type=jnp.float32)
        mixed = jnp.concatenate([mixed[:every, :size], mixed[every:, size:]], axis=0)
        seen.append((top, total, mixed))
        if part == 1:
            (top_r, total_r, mixed_r), (top_b, total_b, mixed_b) = seen
            seen = []
            top = jnp.maximum(top_r, jnp.where(own, top_b, DEAD))
            scale_r = jnp.exp2(top_r - top)
            scale_b = jnp.where(own, jnp.exp2(top_b - top), 0.0)
            total = scale_r * total_r + scale_b * total_b
            inverse = 1.0 / total
            mixed = (scale_r * inverse) * mixed_r + (scale_b * inverse) * mixed_b
            log = top + jnp.log2(total)
            for k in range(2):
                half = log[k * every : (k + 1) * every]
                level = jnp.where(lax.rem(place, heads) == head + k, half, level)
                for j, out in enumerate(outs):
                    at = slice(k * every + j * rows, k * every + (j + 1) * rows)
                    out[(head + k) * rows : (head + k + 1) * rows, :] = mixed[at].astype(out.dtype)
    high = level.astype(jnp.bfloat16).astype(jnp.float32)
    middle = (level - high).astype(jnp.bfloat16).astype(jnp.float32)
    low = level - high - middle
    coded = jnp.where(place < heads, high, jnp.where(place < 2 * heads, middle, low))
    coded = jnp.where(place < 3 * heads, coded, 0.0)
    group = lax.broadcasted_iota(jnp.int32, (SUBLANES, LANES), 1) // period(rows)
    for j, out in enumerate(outs):
        packed = jnp.zeros((SUBLANES, LANES), jnp.float32)
        for g in range(rows // SUBLANES):
            start = j * rows + g * SUBLANES
            packed = jnp.where(group == g, coded[start : start + SUBLANES], packed)
        packed = jnp.concatenate([packed, jnp.zeros_like(packed)], axis=0)
        out[heads * rows :, :] = packed.astype(out.dtype)


def attend(shifts, blocks, caches, after):
    rows, width = blocks[0].shape
    keys = caches[0].shape[1]
    heads = caches[4].shape[0] // 2
    return pl.pallas_call(
        functools.partial(attend_kernel, tuple(shifts), len(after)),
        out_shape=tuple(
            jax.ShapeDtypeStruct((heads * rows + 2 * SUBLANES, width // heads), jnp.bfloat16) for _ in shifts
        ),
        in_specs=[VMEM] * (len(blocks) + len(caches)) + [ANY] * len(after),
        out_specs=[VMEM] * len(shifts),
        compiler_params=pltpu.CompilerParams(vmem_limit_bytes=24 << 20),
        cost_estimate=pl.CostEstimate(
            flops=8 * rows * len(shifts) * width * keys,
            bytes_accessed=8 * keys * width,
            transcendentals=2 * rows * len(shifts) * keys * heads,
        ),
        name="attend",
    )(*blocks, *caches, *after)


def hold_kernel(*refs):
    pass


def hold(arrays):
    return pl.pallas_call(
        hold_kernel,
        out_shape=tuple(jax.ShapeDtypeStruct(array.shape, array.dtype) for array in arrays),
        in_specs=[ANY] * len(arrays),
        out_specs=[ANY] * len(arrays),
        input_output_aliases={i: i for i in range(len(arrays))},
        compiler_params=pltpu.CompilerParams(vmem_limit_bytes=1 << 20),
        cost_estimate=pl.CostEstimate(flops=0, bytes_accessed=4 << 20, transcendentals=0),
        name="hold",
    )(*arrays)


def merge_kernel(*refs):
    out = refs[-1]
    rows, width = out.shape
    heads = (refs[0].shape[0] - 2 * SUBLANES) // rows
    size = width // heads
    lane = lax.rem(lax.broadcasted_iota(jnp.int32, (LANES, width), 0), period(rows))
    head = lax.broadcasted_iota(jnp.int32, (LANES, width), 1) // size
    spread = jnp.where((lax.rem(lane, heads) == head) & (lane < 3 * heads), 1.0, 0.0).astype(jnp.bfloat16)
    group = lax.broadcasted_iota(jnp.int32, (SUBLANES, LANES), 1) // period(rows)
    coded = []
    for ref in refs[:-1]:
        packed = ref[heads * rows :, :].astype(jnp.float32)[:SUBLANES]
        coded += [jnp.where(group == g, packed, 0.0) for g in range(rows // SUBLANES)]
    coded = jnp.concatenate(coded, axis=0).astype(jnp.bfloat16)
    logs = jnp.dot(coded, spread, preferred_element_type=jnp.float32)
    logs = [logs[j * rows : (j + 1) * rows] for j in range(len(refs) - 1)]
    top = functools.reduce(jnp.maximum, logs)
    total = jnp.zeros(out.shape, jnp.float32)
    mixed = jnp.zeros(out.shape, jnp.float32)
    for log, ref in zip(logs, refs[:-1]):
        value = jnp.concatenate([ref[h * rows : (h + 1) * rows, :] for h in range(heads)], axis=1)
        scale = jnp.exp2(log - top)
        total += scale
        mixed += scale * value.astype(jnp.float32)
    out[...] = (mixed / total).astype(out.dtype)


def merge(parts, rows, width):
    return pl.pallas_call(
        merge_kernel,
        out_shape=jax.ShapeDtypeStruct((rows, width), jnp.bfloat16),
        in_specs=[VMEM] * len(parts),
        out_specs=VMEM,
        compiler_params=pltpu.CompilerParams(vmem_limit_bytes=8 << 20),
        name="merge",
    )(*parts)


def shards(queries, root_keys, root_values, branch_keys, branch_values, branch_lengths, branch_ids, slopes):
    count = lax.axis_size("seq")
    rows, width = queries.shape

    def swap(array, shift):
        return lax.ppermute(array, "seq", [(i, i ^ shift) for i in range(count)])

    near, far = (0, 1), tuple(reversed(range(2, count)))
    blocks = {0: queries} | {shift: swap(queries, shift) for shift in far + near[1:]}
    caches = load(root_keys, root_values, branch_keys, branch_values)
    caches += tables(slopes, branch_lengths, branch_ids, rows, root_keys.shape[0], caches[0])
    sent = attend(far, [blocks[s] for s in far], caches, ())
    got = hold([swap(array, shift) for array, shift in zip(sent, far)])
    kept, passed = attend(near, [blocks[s] for s in near], caches, sent[:1])
    return merge([kept, swap(passed, 1), *got], rows, width)


def solution(mesh):
    in_specs = (
        P(("grp", "seq"), "head"),
        P(("grp", "seq"), "head"),
        P(("grp", "seq"), "head"),
        P(("grp", "seq"), "head"),
        P(("grp", "seq"), "head"),
        P(("grp", "seq")),
        P("grp"),
        P("head"),
    )
    out_specs = P(("grp", "seq"), "head")
    return jax.shard_map(shards, mesh=mesh, in_specs=in_specs, out_specs=out_specs, check_vma=False)
```

```python
import functools
import math

import jax
import jax.numpy as jnp
from jax import lax
from jax.experimental import pallas as pl
from jax.experimental.pallas import tpu as pltpu
from jax.sharding import PartitionSpec as P

LOG2E = math.log2(math.e)
DEAD = -1e30
LANES = 128
SUBLANES = 8
ANY = pl.BlockSpec(memory_space=pl.ANY)
HBM = pl.BlockSpec(memory_space=pltpu.HBM)
VMEM = pl.BlockSpec(memory_space=pltpu.VMEM)


def load_kernel(chunks, turned, straight, skipped, *refs):
    sources, outs = refs[: turned + straight], refs[turned + straight + skipped : 2 * (turned + straight) + skipped]
    sems = refs[-1]
    keys, width = sources[0].shape
    rows = keys // chunks
    copies = []
    for i in range(turned):
        for j in range(chunks):
            part = pl.ds(j * rows, rows)
            copies.append(
                pltpu.make_async_copy(sources[i].at[part], refs[-2].at[i, part], sems.at[i * chunks + j])
            )
    for i in range(turned, turned + straight):
        copies.append(pltpu.make_async_copy(sources[i], outs[i], sems.at[turned * chunks + i - turned]))
    for copy in copies:
        copy.start()
    for i in range(turned):
        for j in range(chunks):
            copies[i * chunks + j].wait()
            part = slice(j * rows, (j + 1) * rows)
            for col in range(0, width, LANES):
                outs[i][col : col + LANES, part] = refs[-2][i, part, col : col + LANES].T
    for copy in copies[turned * chunks :]:
        copy.wait()


def load(turned, straight, after, limit):
    chunks = 4
    arrays = (*turned, *straight)
    keys, width = arrays[0].shape
    kind = arrays[0].dtype
    return pl.pallas_call(
        functools.partial(load_kernel, chunks, len(turned), len(straight), len(after)),
        out_shape=tuple(jax.ShapeDtypeStruct((width, keys), kind) for _ in turned)
        + tuple(jax.ShapeDtypeStruct((keys, width), kind) for _ in straight),
        in_specs=[HBM] * len(arrays) + [ANY] * len(after),
        out_specs=(VMEM,) * len(arrays),
        scratch_shapes=[pltpu.VMEM((len(turned), keys, width), kind)] * (len(turned) > 0)
        + [pltpu.SemaphoreType.DMA((len(turned) * chunks + len(straight),))],
        compiler_params=pltpu.CompilerParams(vmem_limit_bytes=limit << 20),
        cost_estimate=pl.CostEstimate(flops=0, bytes_accessed=2 * len(arrays) * keys * width, transcendentals=0),
        name="load",
    )(*arrays, *after)


def column(vector, rows, start):
    wide = jnp.broadcast_to(vector.reshape(1, -1), (rows, vector.shape[0]))
    lane = lax.broadcasted_iota(jnp.int32, wide.shape, 1)
    sub = lax.broadcasted_iota(jnp.int32, wide.shape, 0)
    return jnp.sum(jnp.where(lane == sub + start, wide, jnp.zeros_like(wide)), axis=1, keepdims=True)


def tables_kernel(rows, slopes, lengths, ids, after, bias, mine):
    me = lax.axis_index("seq")
    count = lax.axis_size("seq")
    heads = slopes.shape[0]
    keys = bias.shape[1]
    slope = column(slopes[...], heads, 0) * LOG2E
    spot = lax.broadcasted_iota(jnp.int32, (1, keys), 1)
    place = spot.astype(jnp.float32)
    bias[:heads] = slope * (place + (me * keys - keys * (count + 1)).astype(jnp.float32))
    dead = jnp.where(spot < lengths[...].reshape(1, 1), 0.0, DEAD)
    bias[heads:] = slope * (place - float(keys)) + dead
    mark = jnp.where(ids[...] == me, 1.0, 0.0)
    for shift in range(count):
        at = column(mark, rows, jnp.bitwise_xor(me, shift) * rows)
        mine[shift * rows : (shift + 1) * rows, :] = jnp.broadcast_to(at, (rows, LANES))


def tables(slopes, lengths, ids, rows, keys, after):
    return pl.pallas_call(
        functools.partial(tables_kernel, rows),
        out_shape=(
            jax.ShapeDtypeStruct((2 * slopes.shape[0], keys), jnp.float32),
            jax.ShapeDtypeStruct((ids.shape[0], LANES), jnp.float32),
        ),
        in_specs=[VMEM] * 3 + [ANY],
        out_specs=[VMEM] * 2,
        compiler_params=pltpu.CompilerParams(vmem_limit_bytes=8 << 20),
        name="tables",
    )(slopes, lengths, ids, after)


def period(rows):
    return LANES // (rows // SUBLANES)


def attend_kernel(shifts, skipped, *refs):
    blocks, caches = refs[: len(shifts)], refs[len(shifts) : len(shifts) + 6]
    root_kt, root_v, branch_kt, branch_v, bias, mine = caches
    outs = refs[len(shifts) + 6 + skipped :]
    rows, width = blocks[0].shape
    heads = bias.shape[0] // 2
    size = width // heads
    every = rows * len(shifts)
    factor = LOG2E / math.sqrt(size)
    own = jnp.concatenate([mine[shift * rows : (shift + 1) * rows, :1] for shift in shifts] * 2, axis=0) > 0.5
    zero = jnp.zeros((every, size), blocks[0].dtype)
    units = [(head, part) for head in range(0, heads, 2) for part in (0, 1)]

    def scores(unit):
        head, part = unit
        first = jnp.concatenate([b[:, head * size : (head + 1) * size] for b in blocks], axis=0)
        second = jnp.concatenate([b[:, (head + 1) * size : (head + 2) * size] for b in blocks], axis=0)
        left = jnp.concatenate(
            [jnp.concatenate([first, zero], axis=1), jnp.concatenate([zero, second], axis=1)], axis=0
        )
        key = (root_kt, branch_kt)[part][head * size : (head + 2) * size, :]
        return jnp.dot(left, key, preferred_element_type=jnp.float32)

    ahead = scores(units[0])
    lane = lax.broadcasted_iota(jnp.int32, (every, LANES), 1)
    place = lax.rem(lane, period(rows))
    level = jnp.zeros((every, LANES), jnp.float32)
    seen = []
    for i, (head, part) in enumerate(units):
        raw = ahead
        if i + 1 < len(units):
            ahead = scores(units[i + 1])
        shaped = []
        for k in range(2):
            row = part * heads + head + k
            shaped.append(raw[k * every : (k + 1) * every] * factor + bias[row : row + 1, :])
        shaped = jnp.concatenate(shaped, axis=0)
        top = jnp.max(shaped, axis=1, keepdims=True)
        weight = jnp.exp2(shaped - top)
        total = jnp.sum(weight, axis=1, keepdims=True)
        value = (root_v, branch_v)[part][:, head * size : (head + 2) * size]
        mixed = jnp.dot(weight.astype(value.dtype), value, preferred_element_type=jnp.float32)
        mixed = jnp.concatenate([mixed[:every, :size], mixed[every:, size:]], axis=0)
        seen.append((top, total, mixed))
        if part == 1:
            (top_r, total_r, mixed_r), (top_b, total_b, mixed_b) = seen
            seen = []
            top = jnp.maximum(top_r, jnp.where(own, top_b, DEAD))
            scale_r = jnp.exp2(top_r - top)
            scale_b = jnp.where(own, jnp.exp2(top_b - top), 0.0)
            total = scale_r * total_r + scale_b * total_b
            inverse = 1.0 / total
            mixed = (scale_r * inverse) * mixed_r + (scale_b * inverse) * mixed_b
            log = top + jnp.log2(total)
            for k in range(2):
                half = log[k * every : (k + 1) * every]
                level = jnp.where(lax.rem(place, heads) == head + k, half, level)
                for j, out in enumerate(outs):
                    at = slice(k * every + j * rows, k * every + (j + 1) * rows)
                    out[(head + k) * rows : (head + k + 1) * rows, :] = mixed[at].astype(out.dtype)
    high = level.astype(jnp.bfloat16).astype(jnp.float32)
    middle = (level - high).astype(jnp.bfloat16).astype(jnp.float32)
    low = level - high - middle
    coded = jnp.where(place < heads, high, jnp.where(place < 2 * heads, middle, low))
    coded = jnp.where(place < 3 * heads, coded, 0.0)
    group = lax.broadcasted_iota(jnp.int32, (SUBLANES, LANES), 1) // period(rows)
    for j, out in enumerate(outs):
        packed = jnp.zeros((SUBLANES, LANES), jnp.float32)
        for g in range(rows // SUBLANES):
            start = j * rows + g * SUBLANES
            packed = jnp.where(group == g, coded[start : start + SUBLANES], packed)
        packed = jnp.concatenate([packed, jnp.zeros_like(packed)], axis=0)
        out[heads * rows :, :] = packed.astype(out.dtype)


def attend(shifts, blocks, caches, after):
    rows, width = blocks[0].shape
    keys = caches[0].shape[1]
    heads = caches[4].shape[0] // 2
    return pl.pallas_call(
        functools.partial(attend_kernel, tuple(shifts), len(after)),
        out_shape=tuple(
            jax.ShapeDtypeStruct((heads * rows + 2 * SUBLANES, width // heads), jnp.bfloat16) for _ in shifts
        ),
        in_specs=[VMEM] * (len(blocks) + len(caches)) + [ANY] * len(after),
        out_specs=[VMEM] * len(shifts),
        compiler_params=pltpu.CompilerParams(vmem_limit_bytes=24 << 20),
        cost_estimate=pl.CostEstimate(
            flops=8 * rows * len(shifts) * width * keys,
            bytes_accessed=8 * keys * width,
            transcendentals=2 * rows * len(shifts) * keys * heads,
        ),
        name="attend",
    )(*blocks, *caches, *after)


def hold_kernel(*refs):
    pass


def hold(arrays, after=()):
    return pl.pallas_call(
        hold_kernel,
        out_shape=tuple(jax.ShapeDtypeStruct(array.shape, array.dtype) for array in arrays),
        in_specs=[ANY] * (len(arrays) + len(after)),
        out_specs=[ANY] * len(arrays),
        input_output_aliases={i: i for i in range(len(arrays))},
        compiler_params=pltpu.CompilerParams(vmem_limit_bytes=1 << 20),
        cost_estimate=pl.CostEstimate(flops=0, bytes_accessed=4 << 20, transcendentals=0),
        name="hold",
    )(*arrays, *after)


def merge_kernel(*refs):
    out = refs[-1]
    rows, width = out.shape
    heads = (refs[0].shape[0] - 2 * SUBLANES) // rows
    size = width // heads
    lane = lax.rem(lax.broadcasted_iota(jnp.int32, (LANES, width), 0), period(rows))
    head = lax.broadcasted_iota(jnp.int32, (LANES, width), 1) // size
    spread = jnp.where((lax.rem(lane, heads) == head) & (lane < 3 * heads), 1.0, 0.0).astype(jnp.bfloat16)
    group = lax.broadcasted_iota(jnp.int32, (SUBLANES, LANES), 1) // period(rows)
    coded = []
    for ref in refs[:-1]:
        packed = ref[heads * rows :, :].astype(jnp.float32)[:SUBLANES]
        coded += [jnp.where(group == g, packed, 0.0) for g in range(rows // SUBLANES)]
    coded = jnp.concatenate(coded, axis=0).astype(jnp.bfloat16)
    logs = jnp.dot(coded, spread, preferred_element_type=jnp.float32)
    logs = [logs[j * rows : (j + 1) * rows] for j in range(len(refs) - 1)]
    top = functools.reduce(jnp.maximum, logs)
    total = jnp.zeros(out.shape, jnp.float32)
    mixed = jnp.zeros(out.shape, jnp.float32)
    for log, ref in zip(logs, refs[:-1]):
        value = jnp.concatenate([ref[h * rows : (h + 1) * rows, :] for h in range(heads)], axis=1)
        scale = jnp.exp2(log - top)
        total += scale
        mixed += scale * value.astype(jnp.float32)
    out[...] = (mixed / total).astype(out.dtype)


def merge(parts, rows, width):
    return pl.pallas_call(
        merge_kernel,
        out_shape=jax.ShapeDtypeStruct((rows, width), jnp.bfloat16),
        in_specs=[VMEM] * len(parts),
        out_specs=VMEM,
        compiler_params=pltpu.CompilerParams(vmem_limit_bytes=8 << 20),
        name="merge",
    )(*parts)


def shards(queries, root_keys, root_values, branch_keys, branch_values, branch_lengths, branch_ids, slopes):
    count = lax.axis_size("seq")
    rows, width = queries.shape

    def swap(array, shift):
        return lax.ppermute(array, "seq", [(i, i ^ shift) for i in range(count)])

    near, across = (0, 1), tuple(range(2, count, 2))
    far = across + tuple(shift + 1 for shift in across)
    blocks = {shift: swap(queries, shift) for shift in across}
    blocks[0], blocks[1] = queries, swap(queries, 1)
    root_kt, branch_kt, root_v = load((root_keys, branch_keys), (root_values,), (), 46)
    arrived = hold([blocks[shift] for shift in across], (root_kt, blocks[1]))
    for shift, block in zip(across, arrived):
        blocks[shift], blocks[shift + 1] = block, swap(block, 1)
    bias, mine = tables(slopes, branch_lengths, branch_ids, rows, root_keys.shape[0], root_kt)
    caches = (root_kt, root_v, branch_kt, branch_values, bias, mine)
    sent = attend(far, [blocks[s] for s in far], caches, ())
    got = hold([swap(array, shift) for array, shift in zip(sent, far)])
    kept, passed = attend(near, [blocks[s] for s in near], caches, sent[:1])
    return merge([kept, swap(passed, 1), *got], rows, width)


def solution(mesh):
    in_specs = (
        P(("grp", "seq"), "head"),
        P(("grp", "seq"), "head"),
        P(("grp", "seq"), "head"),
        P(("grp", "seq"), "head"),
        P(("grp", "seq"), "head"),
        P(("grp", "seq")),
        P("grp"),
        P("head"),
    )
    out_specs = P(("grp", "seq"), "head")
    return jax.shard_map(shards, mesh=mesh, in_specs=in_specs, out_specs=out_specs, check_vma=False)
```

```python
import functools
import math

import jax
import jax.numpy as jnp
from jax import lax
from jax.experimental import pallas as pl
from jax.experimental.pallas import tpu as pltpu
from jax.sharding import PartitionSpec as P

LOG2E = math.log2(math.e)
DEAD = -1e30
LANES = 128
SUBLANES = 8
ANY = pl.BlockSpec(memory_space=pl.ANY)
HBM = pl.BlockSpec(memory_space=pltpu.HBM)
VMEM = pl.BlockSpec(memory_space=pltpu.VMEM)


def load_kernel(chunks, turned, straight, skipped, *refs):
    sources, outs = refs[: turned + straight], refs[turned + straight + skipped : 2 * (turned + straight) + skipped]
    sems = refs[-1]
    keys, width = sources[0].shape
    rows = keys // chunks
    copies = []
    for i in range(turned):
        for j in range(chunks):
            part = pl.ds(j * rows, rows)
            copies.append(
                pltpu.make_async_copy(sources[i].at[part], refs[-2].at[i, part], sems.at[i * chunks + j])
            )
    for i in range(turned, turned + straight):
        copies.append(pltpu.make_async_copy(sources[i], outs[i], sems.at[turned * chunks + i - turned]))
    for copy in copies:
        copy.start()
    for i in range(turned):
        for j in range(chunks):
            copies[i * chunks + j].wait()
            part = slice(j * rows, (j + 1) * rows)
            for col in range(0, width, LANES):
                outs[i][col : col + LANES, part] = refs[-2][i, part, col : col + LANES].T
    for copy in copies[turned * chunks :]:
        copy.wait()


def load(turned, straight, after, limit):
    chunks = 4
    arrays = (*turned, *straight)
    keys, width = arrays[0].shape
    kind = arrays[0].dtype
    return pl.pallas_call(
        functools.partial(load_kernel, chunks, len(turned), len(straight), len(after)),
        out_shape=tuple(jax.ShapeDtypeStruct((width, keys), kind) for _ in turned)
        + tuple(jax.ShapeDtypeStruct((keys, width), kind) for _ in straight),
        in_specs=[HBM] * len(arrays) + [ANY] * len(after),
        out_specs=(VMEM,) * len(arrays),
        scratch_shapes=[pltpu.VMEM((len(turned), keys, width), kind)] * (len(turned) > 0)
        + [pltpu.SemaphoreType.DMA((len(turned) * chunks + len(straight),))],
        compiler_params=pltpu.CompilerParams(vmem_limit_bytes=limit << 20),
        cost_estimate=pl.CostEstimate(flops=0, bytes_accessed=2 * len(arrays) * keys * width, transcendentals=0),
        name="load",
    )(*arrays, *after)


def column(vector, rows, start):
    wide = jnp.broadcast_to(vector.reshape(1, -1), (rows, vector.shape[0]))
    lane = lax.broadcasted_iota(jnp.int32, wide.shape, 1)
    sub = lax.broadcasted_iota(jnp.int32, wide.shape, 0)
    return jnp.sum(jnp.where(lane == sub + start, wide, jnp.zeros_like(wide)), axis=1, keepdims=True)


def tables_kernel(rows, slopes, lengths, ids, after, brought, bias, mine):
    me = lax.axis_index("seq")
    count = lax.axis_size("seq")
    heads = slopes.shape[0]
    keys = bias.shape[1]
    slope = column(slopes[...], heads, 0) * LOG2E
    spot = lax.broadcasted_iota(jnp.int32, (1, keys), 1)
    place = spot.astype(jnp.float32)
    bias[:heads] = slope * (place + (me * keys - keys * (count + 1)).astype(jnp.float32))
    dead = jnp.where(spot < lengths[...].reshape(1, 1), 0.0, DEAD)
    bias[heads:] = slope * (place - float(keys)) + dead
    mark = jnp.where(ids[...] == me, 1.0, 0.0)
    for shift in range(count):
        at = column(mark, rows, jnp.bitwise_xor(me, shift) * rows)
        mine[shift * rows : (shift + 1) * rows, :] = jnp.broadcast_to(at, (rows, LANES))


def tables(slopes, lengths, ids, rows, keys, after, brought):
    return pl.pallas_call(
        functools.partial(tables_kernel, rows),
        out_shape=(
            jax.ShapeDtypeStruct((2 * slopes.shape[0], keys), jnp.float32),
            jax.ShapeDtypeStruct((ids.shape[0], LANES), jnp.float32),
        ),
        in_specs=[VMEM] * 3 + [ANY, VMEM],
        out_specs=[VMEM] * 2,
        compiler_params=pltpu.CompilerParams(vmem_limit_bytes=8 << 20),
        name="tables",
    )(slopes, lengths, ids, after, brought)


def period(rows):
    return LANES // (rows // SUBLANES)


def attend_kernel(shifts, skipped, *refs):
    blocks, caches = refs[: len(shifts)], refs[len(shifts) : len(shifts) + 6]
    root_kt, root_v, branch_kt, branch_v, bias, mine = caches
    outs = refs[len(shifts) + 6 + skipped :]
    rows, width = blocks[0].shape
    heads = bias.shape[0] // 2
    size = width // heads
    every = rows * len(shifts)
    factor = LOG2E / math.sqrt(size)
    own = jnp.concatenate([mine[shift * rows : (shift + 1) * rows, :1] for shift in shifts] * 2, axis=0) > 0.5
    units = [(head, part) for head in range(0, heads, 2) for part in (0, 1)]

    def scores(unit):
        head, part = unit
        both = []
        for k in (head, head + 1):
            cols = slice(k * size, (k + 1) * size)
            query = jnp.concatenate([b[:, cols] for b in blocks], axis=0)
            key = (root_kt, branch_kt)[part][cols, :]
            both.append(jnp.dot(query, key, preferred_element_type=jnp.float32))
        return jnp.concatenate(both, axis=0)

    ahead = scores(units[0])
    lane = lax.broadcasted_iota(jnp.int32, (every, LANES), 1)
    place = lax.rem(lane, period(rows))
    level = jnp.zeros((every, LANES), jnp.float32)
    seen = []
    for i, (head, part) in enumerate(units):
        raw = ahead
        if i + 1 < len(units):
            ahead = scores(units[i + 1])
        shaped = []
        for k in range(2):
            row = part * heads + head + k
            shaped.append(raw[k * every : (k + 1) * every] * factor + bias[row : row + 1, :])
        shaped = jnp.concatenate(shaped, axis=0)
        top = jnp.max(shaped, axis=1, keepdims=True)
        weight = jnp.exp2(shaped - top)
        total = jnp.sum(weight, axis=1, keepdims=True)
        value = (root_v, branch_v)[part][:, head * size : (head + 2) * size]
        mixed = jnp.dot(weight.astype(value.dtype), value, preferred_element_type=jnp.float32)
        mixed = jnp.concatenate([mixed[:every, :size], mixed[every:, size:]], axis=0)
        seen.append((top, total, mixed))
        if part == 1:
            (top_r, total_r, mixed_r), (top_b, total_b, mixed_b) = seen
            seen = []
            top = jnp.maximum(top_r, jnp.where(own, top_b, DEAD))
            scale_r = jnp.exp2(top_r - top)
            scale_b = jnp.where(own, jnp.exp2(top_b - top), 0.0)
            total = scale_r * total_r + scale_b * total_b
            inverse = 1.0 / total
            mixed = (scale_r * inverse) * mixed_r + (scale_b * inverse) * mixed_b
            log = top + jnp.log2(total)
            for k in range(2):
                half = log[k * every : (k + 1) * every]
                level = jnp.where(lax.rem(place, heads) == head + k, half, level)
                for j, out in enumerate(outs):
                    at = slice(k * every + j * rows, k * every + (j + 1) * rows)
                    out[(head + k) * rows : (head + k + 1) * rows, :] = mixed[at].astype(out.dtype)
    high = level.astype(jnp.bfloat16).astype(jnp.float32)
    middle = (level - high).astype(jnp.bfloat16).astype(jnp.float32)
    low = level - high - middle
    coded = jnp.where(place < heads, high, jnp.where(place < 2 * heads, middle, low))
    coded = jnp.where(place < 3 * heads, coded, 0.0)
    group = lax.broadcasted_iota(jnp.int32, (SUBLANES, LANES), 1) // period(rows)
    for j, out in enumerate(outs):
        packed = jnp.zeros((SUBLANES, LANES), jnp.float32)
        for g in range(rows // SUBLANES):
            start = j * rows + g * SUBLANES
            packed = jnp.where(group == g, coded[start : start + SUBLANES], packed)
        packed = jnp.concatenate([packed, jnp.zeros_like(packed)], axis=0)
        out[heads * rows :, :] = packed.astype(out.dtype)


def attend(shifts, blocks, caches, after):
    rows, width = blocks[0].shape
    keys = caches[0].shape[1]
    heads = caches[4].shape[0] // 2
    return pl.pallas_call(
        functools.partial(attend_kernel, tuple(shifts), len(after)),
        out_shape=tuple(
            jax.ShapeDtypeStruct((heads * rows + 2 * SUBLANES, width // heads), jnp.bfloat16) for _ in shifts
        ),
        in_specs=[VMEM] * (len(blocks) + len(caches)) + [ANY] * len(after),
        out_specs=[VMEM] * len(shifts),
        compiler_params=pltpu.CompilerParams(vmem_limit_bytes=24 << 20),
        cost_estimate=pl.CostEstimate(
            flops=8 * rows * len(shifts) * width * keys,
            bytes_accessed=8 * keys * width,
            transcendentals=2 * rows * len(shifts) * keys * heads,
        ),
        name="attend",
    )(*blocks, *caches, *after)


def hold_kernel(*refs):
    pass


def hold(arrays, after=()):
    return pl.pallas_call(
        hold_kernel,
        out_shape=tuple(jax.ShapeDtypeStruct(array.shape, array.dtype) for array in arrays),
        in_specs=[ANY] * (len(arrays) + len(after)),
        out_specs=[ANY] * len(arrays),
        input_output_aliases={i: i for i in range(len(arrays))},
        compiler_params=pltpu.CompilerParams(vmem_limit_bytes=1 << 20),
        cost_estimate=pl.CostEstimate(flops=0, bytes_accessed=4 << 20, transcendentals=0),
        name="hold",
    )(*arrays, *after)


def merge_kernel(*refs):
    out = refs[-1]
    rows, width = out.shape
    heads = (refs[0].shape[0] - 2 * SUBLANES) // rows
    size = width // heads
    lane = lax.rem(lax.broadcasted_iota(jnp.int32, (LANES, width), 0), period(rows))
    head = lax.broadcasted_iota(jnp.int32, (LANES, width), 1) // size
    spread = jnp.where((lax.rem(lane, heads) == head) & (lane < 3 * heads), 1.0, 0.0).astype(jnp.bfloat16)
    group = lax.broadcasted_iota(jnp.int32, (SUBLANES, LANES), 1) // period(rows)
    coded = []
    for ref in refs[:-1]:
        packed = ref[heads * rows :, :].astype(jnp.float32)[:SUBLANES]
        coded += [jnp.where(group == g, packed, 0.0) for g in range(rows // SUBLANES)]
    coded = jnp.concatenate(coded, axis=0).astype(jnp.bfloat16)
    logs = jnp.dot(coded, spread, preferred_element_type=jnp.float32)
    logs = [logs[j * rows : (j + 1) * rows] for j in range(len(refs) - 1)]
    top = functools.reduce(jnp.maximum, logs)
    total = jnp.zeros(out.shape, jnp.float32)
    mixed = jnp.zeros(out.shape, jnp.float32)
    for log, ref in zip(logs, refs[:-1]):
        value = jnp.concatenate([ref[h * rows : (h + 1) * rows, :] for h in range(heads)], axis=1)
        scale = jnp.exp2(log - top)
        total += scale
        mixed += scale * value.astype(jnp.float32)
    out[...] = (mixed / total).astype(out.dtype)


def merge(parts, rows, width):
    return pl.pallas_call(
        merge_kernel,
        out_shape=jax.ShapeDtypeStruct((rows, width), jnp.bfloat16),
        in_specs=[VMEM] * len(parts),
        out_specs=VMEM,
        compiler_params=pltpu.CompilerParams(vmem_limit_bytes=8 << 20),
        name="merge",
    )(*parts)


def shards(queries, root_keys, root_values, branch_keys, branch_values, branch_lengths, branch_ids, slopes):
    count = lax.axis_size("seq")
    rows, width = queries.shape

    def swap(array, shift):
        return lax.ppermute(array, "seq", [(i, i ^ shift) for i in range(count)])

    near, across = (0, 1), tuple(range(2, count, 2))
    far = tuple(shift + 1 for shift in across) + across
    blocks = {shift: swap(queries, shift) for shift in across}
    blocks[0], blocks[1] = queries, swap(queries, 1)
    root_kt, branch_kt, root_v = load((root_keys, branch_keys), (root_values,), (), 46)
    arrived = hold([blocks[shift] for shift in across], (root_kt, blocks[1]))
    for shift, block in zip(across, arrived):
        blocks[shift], blocks[shift + 1] = block, swap(block, 1)
    bias, mine = tables(slopes, branch_lengths, branch_ids, rows, root_keys.shape[0], root_kt, branch_values)
    caches = (root_kt, root_v, branch_kt, branch_values, bias, mine)
    sent = attend(far, [blocks[s] for s in far], caches, ())
    got = hold([swap(array, shift) for array, shift in zip(sent, far)])
    kept, passed = attend(near, [blocks[s] for s in near], caches, sent[:1])
    return merge([kept, swap(passed, 1), *got], rows, width)


def solution(mesh):
    in_specs = (
        P(("grp", "seq"), "head"),
        P(("grp", "seq"), "head"),
        P(("grp", "seq"), "head"),
        P(("grp", "seq"), "head"),
        P(("grp", "seq"), "head"),
        P(("grp", "seq")),
        P("grp"),
        P("head"),
    )
    out_specs = P(("grp", "seq"), "head")
    return jax.shard_map(shards, mesh=mesh, in_specs=in_specs, out_specs=out_specs, check_vma=False)
```

```python
import functools
import math

import jax
import jax.numpy as jnp
from jax import lax
from jax.experimental import pallas as pl
from jax.experimental.pallas import tpu as pltpu
from jax.sharding import PartitionSpec as P

LOG2E = math.log2(math.e)
DEAD = -1e30
LANES = 128
SUBLANES = 8
ANY = pl.BlockSpec(memory_space=pl.ANY)
HBM = pl.BlockSpec(memory_space=pltpu.HBM)
VMEM = pl.BlockSpec(memory_space=pltpu.VMEM)


def load_kernel(chunks, turned, straight, skipped, *refs):
    sources, outs = refs[: turned + straight], refs[turned + straight + skipped : 2 * (turned + straight) + skipped]
    sems = refs[-1]
    keys, width = sources[0].shape
    rows = keys // chunks
    copies = []
    for i in range(turned):
        for j in range(chunks):
            part = pl.ds(j * rows, rows)
            copies.append(
                pltpu.make_async_copy(sources[i].at[part], refs[-2].at[i, part], sems.at[i * chunks + j])
            )
    for i in range(turned, turned + straight):
        copies.append(pltpu.make_async_copy(sources[i], outs[i], sems.at[turned * chunks + i - turned]))
    for copy in copies:
        copy.start()
    for i in range(turned):
        for j in range(chunks):
            copies[i * chunks + j].wait()
            part = slice(j * rows, (j + 1) * rows)
            for col in range(0, width, LANES):
                outs[i][col : col + LANES, part] = refs[-2][i, part, col : col + LANES].T
    for copy in copies[turned * chunks :]:
        copy.wait()


def load(turned, straight, after, limit):
    chunks = 4
    arrays = (*turned, *straight)
    keys, width = arrays[0].shape
    kind = arrays[0].dtype
    return pl.pallas_call(
        functools.partial(load_kernel, chunks, len(turned), len(straight), len(after)),
        out_shape=tuple(jax.ShapeDtypeStruct((width, keys), kind) for _ in turned)
        + tuple(jax.ShapeDtypeStruct((keys, width), kind) for _ in straight),
        in_specs=[HBM] * len(arrays) + [ANY] * len(after),
        out_specs=(VMEM,) * len(arrays),
        scratch_shapes=[pltpu.VMEM((len(turned), keys, width), kind)] * (len(turned) > 0)
        + [pltpu.SemaphoreType.DMA((len(turned) * chunks + len(straight),))],
        compiler_params=pltpu.CompilerParams(vmem_limit_bytes=limit << 20),
        cost_estimate=pl.CostEstimate(flops=0, bytes_accessed=2 * len(arrays) * keys * width, transcendentals=0),
        name="load",
    )(*arrays, *after)


def column(vector, rows, start):
    wide = jnp.broadcast_to(vector.reshape(1, -1), (rows, vector.shape[0]))
    lane = lax.broadcasted_iota(jnp.int32, wide.shape, 1)
    sub = lax.broadcasted_iota(jnp.int32, wide.shape, 0)
    return jnp.sum(jnp.where(lane == sub + start, wide, jnp.zeros_like(wide)), axis=1, keepdims=True)


def tables_kernel(rows, slopes, lengths, ids, after, brought, bias, mine):
    me = lax.axis_index("seq")
    count = lax.axis_size("seq")
    heads = slopes.shape[0]
    keys = bias.shape[1]
    slope = column(slopes[...], heads, 0) * LOG2E
    spot = lax.broadcasted_iota(jnp.int32, (1, keys), 1)
    place = spot.astype(jnp.float32)
    bias[:heads] = slope * (place + (me * keys - keys * (count + 1)).astype(jnp.float32))
    dead = jnp.where(spot < lengths[...].reshape(1, 1), 0.0, DEAD)
    bias[heads:] = slope * (place - float(keys)) + dead
    mark = jnp.where(ids[...] == me, 1.0, 0.0)
    for shift in range(count):
        at = column(mark, rows, jnp.bitwise_xor(me, shift) * rows)
        mine[shift * rows : (shift + 1) * rows, :] = jnp.broadcast_to(at, (rows, LANES))


def tables(slopes, lengths, ids, rows, keys, after, brought):
    return pl.pallas_call(
        functools.partial(tables_kernel, rows),
        out_shape=(
            jax.ShapeDtypeStruct((2 * slopes.shape[0], keys), jnp.float32),
            jax.ShapeDtypeStruct((ids.shape[0], LANES), jnp.float32),
        ),
        in_specs=[VMEM] * 3 + [ANY, VMEM],
        out_specs=[VMEM] * 2,
        compiler_params=pltpu.CompilerParams(vmem_limit_bytes=8 << 20),
        name="tables",
    )(slopes, lengths, ids, after, brought)


def period(rows):
    return LANES // (rows // SUBLANES)


def attend_kernel(shifts, skipped, *refs):
    blocks, caches = refs[: len(shifts)], refs[len(shifts) : len(shifts) + 6]
    root_kt, root_v, branch_kt, branch_v, bias, mine = caches
    outs = refs[len(shifts) + 6 + skipped :]
    rows, width = blocks[0].shape
    heads = bias.shape[0] // 2
    size = width // heads
    every = rows * len(shifts)
    factor = LOG2E / math.sqrt(size)
    own = jnp.concatenate([mine[shift * rows : (shift + 1) * rows, :1] for shift in shifts] * 2, axis=0) > 0.5
    units = [(head, part) for head in range(0, heads, 2) for part in (0, 1)]

    def scores(unit):
        head, part = unit
        both = []
        for k in (head, head + 1):
            cols = slice(k * size, (k + 1) * size)
            query = jnp.concatenate([b[:, cols] for b in blocks], axis=0)
            key = (root_kt, branch_kt)[part][cols, :]
            both.append(jnp.dot(query, key, preferred_element_type=jnp.float32))
        return jnp.concatenate(both, axis=0)

    ahead = scores(units[0])
    lane = lax.broadcasted_iota(jnp.int32, (every, LANES), 1)
    place = lax.rem(lane, period(rows))
    level = jnp.zeros((every, LANES), jnp.float32)
    seen = []
    for i, (head, part) in enumerate(units):
        raw = ahead
        if i + 1 < len(units):
            ahead = scores(units[i + 1])
        shaped = []
        for k in range(2):
            row = part * heads + head + k
            shaped.append(raw[k * every : (k + 1) * every] * factor + bias[row : row + 1, :])
        shaped = jnp.concatenate(shaped, axis=0)
        top = jnp.max(shaped, axis=1, keepdims=True)
        weight = jnp.exp2(shaped - top)
        total = jnp.sum(weight, axis=1, keepdims=True)
        value = (root_v, branch_v)[part][:, head * size : (head + 2) * size]
        mixed = jnp.dot(weight.astype(value.dtype), value, preferred_element_type=jnp.float32)
        mixed = jnp.concatenate([mixed[:every, :size], mixed[every:, size:]], axis=0)
        seen.append((top, total, mixed))
        if part == 1:
            (top_r, total_r, mixed_r), (top_b, total_b, mixed_b) = seen
            seen = []
            top = jnp.maximum(top_r, jnp.where(own, top_b, DEAD))
            scale_r = jnp.exp2(top_r - top)
            scale_b = jnp.where(own, jnp.exp2(top_b - top), 0.0)
            total = scale_r * total_r + scale_b * total_b
            inverse = 1.0 / total
            mixed = (scale_r * inverse) * mixed_r + (scale_b * inverse) * mixed_b
            log = top + jnp.log2(total)
            for k in range(2):
                half = log[k * every : (k + 1) * every]
                level = jnp.where(lax.rem(place, heads) == head + k, half, level)
                for j, out in enumerate(outs):
                    at = slice(k * every + j * rows, k * every + (j + 1) * rows)
                    out[(head + k) * rows : (head + k + 1) * rows, :] = mixed[at].astype(out.dtype)
    high = level.astype(jnp.bfloat16).astype(jnp.float32)
    middle = (level - high).astype(jnp.bfloat16).astype(jnp.float32)
    low = level - high - middle
    coded = jnp.where(place < heads, high, jnp.where(place < 2 * heads, middle, low))
    coded = jnp.where(place < 3 * heads, coded, 0.0)
    group = lax.broadcasted_iota(jnp.int32, (SUBLANES, LANES), 1) // period(rows)
    for j, out in enumerate(outs):
        packed = jnp.zeros((SUBLANES, LANES), jnp.float32)
        for g in range(rows // SUBLANES):
            start = j * rows + g * SUBLANES
            packed = jnp.where(group == g, coded[start : start + SUBLANES], packed)
        packed = jnp.concatenate([packed, jnp.zeros_like(packed)], axis=0)
        out[heads * rows :, :] = packed.astype(out.dtype)


def attend(shifts, blocks, caches, after):
    rows, width = blocks[0].shape
    keys = caches[0].shape[1]
    heads = caches[4].shape[0] // 2
    return pl.pallas_call(
        functools.partial(attend_kernel, tuple(shifts), len(after)),
        out_shape=tuple(
            jax.ShapeDtypeStruct((heads * rows + 2 * SUBLANES, width // heads), jnp.bfloat16) for _ in shifts
        ),
        in_specs=[VMEM] * (len(blocks) + len(caches)) + [ANY] * len(after),
        out_specs=[VMEM] * len(shifts),
        compiler_params=pltpu.CompilerParams(vmem_limit_bytes=24 << 20),
        cost_estimate=pl.CostEstimate(
            flops=8 * rows * len(shifts) * width * keys,
            bytes_accessed=8 * keys * width,
            transcendentals=2 * rows * len(shifts) * keys * heads,
        ),
        name="attend",
    )(*blocks, *caches, *after)


def hold_kernel(*refs):
    pass


def hold(arrays, after=(), spent=4 << 20):
    return pl.pallas_call(
        hold_kernel,
        out_shape=tuple(jax.ShapeDtypeStruct(array.shape, array.dtype) for array in arrays),
        in_specs=[ANY] * (len(arrays) + len(after)),
        out_specs=[ANY] * len(arrays),
        input_output_aliases={i: i for i in range(len(arrays))},
        compiler_params=pltpu.CompilerParams(vmem_limit_bytes=1 << 20),
        cost_estimate=pl.CostEstimate(flops=0, bytes_accessed=spent, transcendentals=0),
        name="hold",
    )(*arrays, *after)


def spread_of(rows, heads, size):
    lane = lax.rem(lax.broadcasted_iota(jnp.int32, (LANES, heads * size), 0), period(rows))
    head = lax.broadcasted_iota(jnp.int32, (LANES, heads * size), 1) // size
    return jnp.where((lax.rem(lane, heads) == head) & (lane < 3 * heads), 1.0, 0.0).astype(jnp.bfloat16)


def opened(refs, rows, heads, spread):
    group = lax.broadcasted_iota(jnp.int32, (SUBLANES, LANES), 1) // period(rows)
    coded = []
    for ref in refs:
        packed = ref[heads * rows :, :].astype(jnp.float32)[:SUBLANES]
        coded += [jnp.where(group == g, packed, 0.0) for g in range(rows // SUBLANES)]
    coded = jnp.concatenate(coded, axis=0).astype(jnp.bfloat16)
    logs = jnp.dot(coded, spread, preferred_element_type=jnp.float32)
    values = [jnp.concatenate([ref[h * rows : (h + 1) * rows, :] for h in range(heads)], axis=1) for ref in refs]
    return [(value.astype(jnp.float32), logs[j * rows : (j + 1) * rows]) for j, value in enumerate(values)]


def gather_kernel(rows, heads, *refs):
    *messages, mixed, total, top, spread = refs
    spread[...] = spread_of(rows, heads, messages[0].shape[1])
    parts = opened(messages, rows, heads, spread[...])
    level = functools.reduce(jnp.maximum, [log for _, log in parts])
    scales = [jnp.exp2(log - level) for _, log in parts]
    top[...] = level
    total[...] = functools.reduce(jnp.add, scales)
    mixed[...] = functools.reduce(jnp.add, [scale * value for scale, (value, _) in zip(scales, parts)])


def gather(parts, rows, width):
    wide = jax.ShapeDtypeStruct((rows, width), jnp.float32)
    heads = width // parts[0].shape[1]
    return pl.pallas_call(
        functools.partial(gather_kernel, rows, heads),
        out_shape=(wide, wide, wide, jax.ShapeDtypeStruct((LANES, width), jnp.bfloat16)),
        in_specs=[VMEM] * len(parts),
        out_specs=(VMEM,) * 4,
        compiler_params=pltpu.CompilerParams(vmem_limit_bytes=8 << 20),
        cost_estimate=pl.CostEstimate(flops=0, bytes_accessed=1 << 20, transcendentals=0),
        name="gather",
    )(*parts)


def merge_kernel(mixed, total, top, spread, *refs):
    out = refs[-1]
    rows, width = out.shape
    parts = opened(refs[:-1], rows, width // refs[0].shape[1], spread[...])
    level = functools.reduce(jnp.maximum, [log for _, log in parts], top[...])
    scale = jnp.exp2(top[...] - level)
    whole, sums = scale * mixed[...], scale * total[...]
    for value, log in parts:
        scale = jnp.exp2(log - level)
        whole += scale * value
        sums += scale
    out[...] = (whole / sums).astype(out.dtype)


def merge(gathered, last, rows, width):
    return pl.pallas_call(
        merge_kernel,
        out_shape=jax.ShapeDtypeStruct((rows, width), jnp.bfloat16),
        in_specs=[VMEM] * (4 + len(last)),
        out_specs=VMEM,
        compiler_params=pltpu.CompilerParams(vmem_limit_bytes=8 << 20),
        name="merge",
    )(*gathered, *last)


def shards(queries, root_keys, root_values, branch_keys, branch_values, branch_lengths, branch_ids, slopes):
    count = lax.axis_size("seq")
    rows, width = queries.shape

    def swap(array, shift):
        return lax.ppermute(array, "seq", [(i, i ^ shift) for i in range(count)])

    near, across = (0, 1), tuple(range(2, count, 2))
    far = tuple(shift + 1 for shift in across) + across
    blocks = {shift: swap(queries, shift) for shift in across}
    blocks[0], blocks[1] = queries, swap(queries, 1)
    root_kt, branch_kt, root_v = load((root_keys, branch_keys), (root_values,), (), 46)
    arrived = hold([blocks[shift] for shift in across], (root_kt, blocks[1]))
    for shift, block in zip(across, arrived):
        blocks[shift], blocks[shift + 1] = block, swap(block, 1)
    bias, mine = tables(slopes, branch_lengths, branch_ids, rows, root_keys.shape[0], root_kt, branch_values)
    caches = (root_kt, root_v, branch_kt, branch_values, bias, mine)
    sent = attend(far, [blocks[s] for s in far], caches, ())
    got = [swap(array, shift) for array, shift in zip(sent, far)]
    kept, passed = attend(near, [blocks[s] for s in near], caches, sent[:1])
    gathered = gather([kept, *hold(got[1:])], rows, width)
    (last,) = hold(got[:1], gathered[:1])
    return merge(gathered, [last, swap(passed, 1)], rows, width)


def solution(mesh):
    in_specs = (
        P(("grp", "seq"), "head"),
        P(("grp", "seq"), "head"),
        P(("grp", "seq"), "head"),
        P(("grp", "seq"), "head"),
        P(("grp", "seq"), "head"),
        P(("grp", "seq")),
        P("grp"),
        P("head"),
    )
    out_specs = P(("grp", "seq"), "head")
    return jax.shard_map(shards, mesh=mesh, in_specs=in_specs, out_specs=out_specs, check_vma=False)
```

```python
import functools
import math

import jax
import jax.numpy as jnp
from jax import lax
from jax.experimental import pallas as pl
from jax.experimental.pallas import tpu as pltpu
from jax.sharding import PartitionSpec as P

LOG2E = math.log2(math.e)
DEAD = -1e30
LANES = 128
SUBLANES = 8
ANY = pl.BlockSpec(memory_space=pl.ANY)
HBM = pl.BlockSpec(memory_space=pltpu.HBM)
VMEM = pl.BlockSpec(memory_space=pltpu.VMEM)


def load_kernel(chunks, turned, straight, skipped, *refs):
    sources, outs = refs[: turned + straight], refs[turned + straight + skipped : 2 * (turned + straight) + skipped]
    sems = refs[-1]
    keys, width = sources[0].shape
    rows = keys // chunks
    copies = []
    for i in range(turned):
        for j in range(chunks):
            part = pl.ds(j * rows, rows)
            copies.append(
                pltpu.make_async_copy(sources[i].at[part], refs[-2].at[i, part], sems.at[i * chunks + j])
            )
    for i in range(turned, turned + straight):
        copies.append(pltpu.make_async_copy(sources[i], outs[i], sems.at[turned * chunks + i - turned]))
    for copy in copies[: turned * chunks]:
        copy.start()
    for i in range(turned):
        for j in range(chunks):
            copies[i * chunks + j].wait()
            if i == j == 0:
                for copy in copies[turned * chunks :]:
                    copy.start()
            part = slice(j * rows, (j + 1) * rows)
            for col in range(0, width, LANES):
                outs[i][col : col + LANES, part] = refs[-2][i, part, col : col + LANES].T
    for copy in copies[turned * chunks :]:
        copy.wait()


def load(turned, straight, after, limit):
    chunks = 4
    arrays = (*turned, *straight)
    keys, width = arrays[0].shape
    kind = arrays[0].dtype
    return pl.pallas_call(
        functools.partial(load_kernel, chunks, len(turned), len(straight), len(after)),
        out_shape=tuple(jax.ShapeDtypeStruct((width, keys), kind) for _ in turned)
        + tuple(jax.ShapeDtypeStruct((keys, width), kind) for _ in straight),
        in_specs=[HBM] * len(arrays) + [ANY] * len(after),
        out_specs=(VMEM,) * len(arrays),
        scratch_shapes=[pltpu.VMEM((len(turned), keys, width), kind)] * (len(turned) > 0)
        + [pltpu.SemaphoreType.DMA((len(turned) * chunks + len(straight),))],
        compiler_params=pltpu.CompilerParams(vmem_limit_bytes=limit << 20),
        cost_estimate=pl.CostEstimate(flops=0, bytes_accessed=2 * len(arrays) * keys * width, transcendentals=0),
        name="load",
    )(*arrays, *after)


def column(vector, rows, start):
    wide = jnp.broadcast_to(vector.reshape(1, -1), (rows, vector.shape[0]))
    lane = lax.broadcasted_iota(jnp.int32, wide.shape, 1)
    sub = lax.broadcasted_iota(jnp.int32, wide.shape, 0)
    return jnp.sum(jnp.where(lane == sub + start, wide, jnp.zeros_like(wide)), axis=1, keepdims=True)


def tables_kernel(rows, slopes, lengths, ids, after, brought, bias, mine):
    me = lax.axis_index("seq")
    count = lax.axis_size("seq")
    heads = slopes.shape[0]
    keys = bias.shape[1]
    slope = column(slopes[...], heads, 0) * LOG2E
    spot = lax.broadcasted_iota(jnp.int32, (1, keys), 1)
    place = spot.astype(jnp.float32)
    bias[:heads] = slope * (place + (me * keys - keys * (count + 1)).astype(jnp.float32))
    dead = jnp.where(spot < lengths[...].reshape(1, 1), 0.0, DEAD)
    bias[heads:] = slope * (place - float(keys)) + dead
    mark = jnp.where(ids[...] == me, 1.0, 0.0)
    for shift in range(count):
        at = column(mark, rows, jnp.bitwise_xor(me, shift) * rows)
        mine[shift * rows : (shift + 1) * rows, :] = jnp.broadcast_to(at, (rows, LANES))


def tables(slopes, lengths, ids, rows, keys, after, brought):
    return pl.pallas_call(
        functools.partial(tables_kernel, rows),
        out_shape=(
            jax.ShapeDtypeStruct((2 * slopes.shape[0], keys), jnp.float32),
            jax.ShapeDtypeStruct((ids.shape[0], LANES), jnp.float32),
        ),
        in_specs=[VMEM] * 3 + [ANY, VMEM],
        out_specs=[VMEM] * 2,
        compiler_params=pltpu.CompilerParams(vmem_limit_bytes=8 << 20),
        name="tables",
    )(slopes, lengths, ids, after, brought)


def period(rows):
    return LANES // (rows // SUBLANES)


def attend_kernel(shifts, skipped, *refs):
    blocks, caches = refs[: len(shifts)], refs[len(shifts) : len(shifts) + 6]
    root_kt, root_v, branch_kt, branch_v, bias, mine = caches
    outs = refs[len(shifts) + 6 + skipped :]
    rows, width = blocks[0].shape
    heads = bias.shape[0] // 2
    size = width // heads
    every = rows * len(shifts)
    factor = LOG2E / math.sqrt(size)
    own = jnp.concatenate([mine[shift * rows : (shift + 1) * rows, :1] for shift in shifts] * 2, axis=0) > 0.5
    units = [(head, part) for head in range(0, heads, 2) for part in (0, 1)]

    def scores(unit):
        head, part = unit
        both = []
        for k in (head, head + 1):
            cols = slice(k * size, (k + 1) * size)
            query = jnp.concatenate([b[:, cols] for b in blocks], axis=0)
            key = (root_kt, branch_kt)[part][cols, :]
            both.append(jnp.dot(query, key, preferred_element_type=jnp.float32))
        return jnp.concatenate(both, axis=0)

    ahead = scores(units[0])
    lane = lax.broadcasted_iota(jnp.int32, (every, LANES), 1)
    place = lax.rem(lane, period(rows))
    level = jnp.zeros((every, LANES), jnp.float32)
    seen = []
    for i, (head, part) in enumerate(units):
        raw = ahead
        if i + 1 < len(units):
            ahead = scores(units[i + 1])
        shaped = []
        for k in range(2):
            row = part * heads + head + k
            shaped.append(raw[k * every : (k + 1) * every] * factor + bias[row : row + 1, :])
        shaped = jnp.concatenate(shaped, axis=0)
        top = jnp.max(shaped, axis=1, keepdims=True)
        weight = jnp.exp2(shaped - top)
        total = jnp.sum(weight, axis=1, keepdims=True)
        value = (root_v, branch_v)[part][:, head * size : (head + 2) * size]
        mixed = jnp.dot(weight.astype(value.dtype), value, preferred_element_type=jnp.float32)
        mixed = jnp.concatenate([mixed[:every, :size], mixed[every:, size:]], axis=0)
        seen.append((top, total, mixed))
        if part == 1:
            (top_r, total_r, mixed_r), (top_b, total_b, mixed_b) = seen
            seen = []
            top = jnp.maximum(top_r, jnp.where(own, top_b, DEAD))
            scale_r = jnp.exp2(top_r - top)
            scale_b = jnp.where(own, jnp.exp2(top_b - top), 0.0)
            total = scale_r * total_r + scale_b * total_b
            inverse = 1.0 / total
            mixed = (scale_r * inverse) * mixed_r + (scale_b * inverse) * mixed_b
            log = top + jnp.log2(total)
            for k in range(2):
                half = log[k * every : (k + 1) * every]
                level = jnp.where(lax.rem(place, heads) == head + k, half, level)
                for j, out in enumerate(outs):
                    at = slice(k * every + j * rows, k * every + (j + 1) * rows)
                    out[(head + k) * rows : (head + k + 1) * rows, :] = mixed[at].astype(out.dtype)
    high = level.astype(jnp.bfloat16).astype(jnp.float32)
    middle = (level - high).astype(jnp.bfloat16).astype(jnp.float32)
    low = level - high - middle
    coded = jnp.where(place < heads, high, jnp.where(place < 2 * heads, middle, low))
    coded = jnp.where(place < 3 * heads, coded, 0.0)
    group = lax.broadcasted_iota(jnp.int32, (SUBLANES, LANES), 1) // period(rows)
    for j, out in enumerate(outs):
        packed = jnp.zeros((SUBLANES, LANES), jnp.float32)
        for g in range(rows // SUBLANES):
            start = j * rows + g * SUBLANES
            packed = jnp.where(group == g, coded[start : start + SUBLANES], packed)
        packed = jnp.concatenate([packed, jnp.zeros_like(packed)], axis=0)
        out[heads * rows :, :] = packed.astype(out.dtype)


def attend(shifts, blocks, caches, after):
    rows, width = blocks[0].shape
    keys = caches[0].shape[1]
    heads = caches[4].shape[0] // 2
    return pl.pallas_call(
        functools.partial(attend_kernel, tuple(shifts), len(after)),
        out_shape=tuple(
            jax.ShapeDtypeStruct((heads * rows + 2 * SUBLANES, width // heads), jnp.bfloat16) for _ in shifts
        ),
        in_specs=[VMEM] * (len(blocks) + len(caches)) + [ANY] * len(after),
        out_specs=[VMEM] * len(shifts),
        compiler_params=pltpu.CompilerParams(vmem_limit_bytes=24 << 20),
        cost_estimate=pl.CostEstimate(
            flops=8 * rows * len(shifts) * width * keys,
            bytes_accessed=8 * keys * width,
            transcendentals=2 * rows * len(shifts) * keys * heads,
        ),
        name="attend",
    )(*blocks, *caches, *after)


def hold_kernel(*refs):
    pass


def hold(arrays, after=(), spent=4 << 20):
    return pl.pallas_call(
        hold_kernel,
        out_shape=tuple(jax.ShapeDtypeStruct(array.shape, array.dtype) for array in arrays),
        in_specs=[ANY] * (len(arrays) + len(after)),
        out_specs=[ANY] * len(arrays),
        input_output_aliases={i: i for i in range(len(arrays))},
        compiler_params=pltpu.CompilerParams(vmem_limit_bytes=1 << 20),
        cost_estimate=pl.CostEstimate(flops=0, bytes_accessed=spent, transcendentals=0),
        name="hold",
    )(*arrays, *after)


def spread_of(rows, heads, size):
    lane = lax.rem(lax.broadcasted_iota(jnp.int32, (LANES, heads * size), 0), period(rows))
    head = lax.broadcasted_iota(jnp.int32, (LANES, heads * size), 1) // size
    return jnp.where((lax.rem(lane, heads) == head) & (lane < 3 * heads), 1.0, 0.0).astype(jnp.bfloat16)


def opened(refs, rows, heads, spread):
    group = lax.broadcasted_iota(jnp.int32, (SUBLANES, LANES), 1) // period(rows)
    coded = []
    for ref in refs:
        packed = ref[heads * rows :, :].astype(jnp.float32)[:SUBLANES]
        coded += [jnp.where(group == g, packed, 0.0) for g in range(rows // SUBLANES)]
    coded = jnp.concatenate(coded, axis=0).astype(jnp.bfloat16)
    logs = jnp.dot(coded, spread, preferred_element_type=jnp.float32)
    values = [jnp.concatenate([ref[h * rows : (h + 1) * rows, :] for h in range(heads)], axis=1) for ref in refs]
    return [(value.astype(jnp.float32), logs[j * rows : (j + 1) * rows]) for j, value in enumerate(values)]


def gather_kernel(rows, heads, *refs):
    *messages, mixed, total, top, spread = refs
    spread[...] = spread_of(rows, heads, messages[0].shape[1])
    parts = opened(messages, rows, heads, spread[...])
    level = functools.reduce(jnp.maximum, [log for _, log in parts])
    scales = [jnp.exp2(log - level) for _, log in parts]
    top[...] = level
    total[...] = functools.reduce(jnp.add, scales)
    mixed[...] = functools.reduce(jnp.add, [scale * value for scale, (value, _) in zip(scales, parts)])


def gather(parts, rows, width):
    wide = jax.ShapeDtypeStruct((rows, width), jnp.float32)
    heads = width // parts[0].shape[1]
    return pl.pallas_call(
        functools.partial(gather_kernel, rows, heads),
        out_shape=(wide, wide, wide, jax.ShapeDtypeStruct((LANES, width), jnp.bfloat16)),
        in_specs=[VMEM] * len(parts),
        out_specs=(VMEM,) * 4,
        compiler_params=pltpu.CompilerParams(vmem_limit_bytes=8 << 20),
        cost_estimate=pl.CostEstimate(flops=0, bytes_accessed=1 << 20, transcendentals=0),
        name="gather",
    )(*parts)


def merge_kernel(mixed, total, top, spread, *refs):
    out = refs[-1]
    rows, width = out.shape
    parts = opened(refs[:-1], rows, width // refs[0].shape[1], spread[...])
    level = functools.reduce(jnp.maximum, [log for _, log in parts], top[...])
    scale = jnp.exp2(top[...] - level)
    whole, sums = scale * mixed[...], scale * total[...]
    for value, log in parts:
        scale = jnp.exp2(log - level)
        whole += scale * value
        sums += scale
    out[...] = (whole / sums).astype(out.dtype)


def merge(gathered, last, rows, width):
    return pl.pallas_call(
        merge_kernel,
        out_shape=jax.ShapeDtypeStruct((rows, width), jnp.bfloat16),
        in_specs=[VMEM] * (4 + len(last)),
        out_specs=VMEM,
        compiler_params=pltpu.CompilerParams(vmem_limit_bytes=8 << 20),
        name="merge",
    )(*gathered, *last)


def shards(queries, root_keys, root_values, branch_keys, branch_values, branch_lengths, branch_ids, slopes):
    count = lax.axis_size("seq")
    rows, width = queries.shape

    def swap(array, shift):
        return lax.ppermute(array, "seq", [(i, i ^ shift) for i in range(count)])

    near, across = (0, 1), tuple(range(2, count, 2))
    far = tuple(shift + 1 for shift in across) + across
    blocks = {shift: swap(queries, shift) for shift in across}
    blocks[0], blocks[1] = queries, swap(queries, 1)
    root_kt, branch_kt, root_v = load((root_keys, branch_keys), (root_values,), (), 46)
    arrived = hold([blocks[shift] for shift in across], (root_kt, blocks[1]))
    for shift, block in zip(across, arrived):
        blocks[shift], blocks[shift + 1] = block, swap(block, 1)
    bias, mine = tables(slopes, branch_lengths, branch_ids, rows, root_keys.shape[0], root_kt, branch_values)
    caches = (root_kt, root_v, branch_kt, branch_values, bias, mine)
    sent = attend(far, [blocks[s] for s in far], caches, ())
    got = [swap(array, shift) for array, shift in zip(sent, far)]
    kept, passed = attend(near, [blocks[s] for s in near], caches, sent[:1])
    gathered = gather([kept, *hold(got[1:])], rows, width)
    (last,) = hold(got[:1], gathered[:1])
    return merge(gathered, [last, swap(passed, 1)], rows, width)


def solution(mesh):
    in_specs = (
        P(("grp", "seq"), "head"),
        P(("grp", "seq"), "head"),
        P(("grp", "seq"), "head"),
        P(("grp", "seq"), "head"),
        P(("grp", "seq"), "head"),
        P(("grp", "seq")),
        P("grp"),
        P("head"),
    )
    out_specs = P(("grp", "seq"), "head")
    return jax.shard_map(shards, mesh=mesh, in_specs=in_specs, out_specs=out_specs, check_vma=False)
```

```python
import functools
import math

import jax
import jax.numpy as jnp
from jax import lax
from jax.experimental import pallas as pl
from jax.experimental.pallas import tpu as pltpu
from jax.sharding import PartitionSpec as P

LOG2E = math.log2(math.e)
DEAD = -1e30
LANES = 128
SUBLANES = 8
ANY = pl.BlockSpec(memory_space=pl.ANY)
HBM = pl.BlockSpec(memory_space=pltpu.HBM)
VMEM = pl.BlockSpec(memory_space=pltpu.VMEM)


def load_kernel(chunks, turned, straight, skipped, *refs):
    sources, outs = refs[: turned + straight], refs[turned + straight + skipped : 2 * (turned + straight) + skipped]
    sems = refs[-1]
    keys, width = sources[0].shape
    rows = keys // chunks
    copies = []
    for i in range(turned):
        for j in range(chunks):
            part = pl.ds(j * rows, rows)
            copies.append(
                pltpu.make_async_copy(sources[i].at[part], refs[-2].at[i, part], sems.at[i * chunks + j])
            )
    for i in range(turned, turned + straight):
        copies.append(pltpu.make_async_copy(sources[i], outs[i], sems.at[turned * chunks + i - turned]))
    for copy in copies[: turned * chunks]:
        copy.start()
    for i in range(turned):
        for j in range(chunks):
            copies[i * chunks + j].wait()
            if i == j == 0:
                for copy in copies[turned * chunks :]:
                    copy.start()
            part = slice(j * rows, (j + 1) * rows)
            for col in range(0, width, LANES):
                outs[i][col : col + LANES, part] = refs[-2][i, part, col : col + LANES].T
    for copy in copies[turned * chunks :]:
        copy.wait()


def load(turned, straight, after, limit):
    chunks = 8
    arrays = (*turned, *straight)
    keys, width = arrays[0].shape
    kind = arrays[0].dtype
    return pl.pallas_call(
        functools.partial(load_kernel, chunks, len(turned), len(straight), len(after)),
        out_shape=tuple(jax.ShapeDtypeStruct((width, keys), kind) for _ in turned)
        + tuple(jax.ShapeDtypeStruct((keys, width), kind) for _ in straight),
        in_specs=[HBM] * len(arrays) + [ANY] * len(after),
        out_specs=(VMEM,) * len(arrays),
        scratch_shapes=[pltpu.VMEM((len(turned), keys, width), kind)] * (len(turned) > 0)
        + [pltpu.SemaphoreType.DMA((len(turned) * chunks + len(straight),))],
        compiler_params=pltpu.CompilerParams(vmem_limit_bytes=limit << 20),
        cost_estimate=pl.CostEstimate(flops=0, bytes_accessed=2 * len(arrays) * keys * width, transcendentals=0),
        name="load",
    )(*arrays, *after)


def column(vector, rows, start):
    wide = jnp.broadcast_to(vector.reshape(1, -1), (rows, vector.shape[0]))
    lane = lax.broadcasted_iota(jnp.int32, wide.shape, 1)
    sub = lax.broadcasted_iota(jnp.int32, wide.shape, 0)
    return jnp.sum(jnp.where(lane == sub + start, wide, jnp.zeros_like(wide)), axis=1, keepdims=True)


def tables_kernel(rows, slopes, lengths, ids, after, brought, bias, mine):
    me = lax.axis_index("seq")
    count = lax.axis_size("seq")
    heads = slopes.shape[0]
    keys = bias.shape[1]
    slope = column(slopes[...], heads, 0) * LOG2E
    spot = lax.broadcasted_iota(jnp.int32, (1, keys), 1)
    place = spot.astype(jnp.float32)
    bias[:heads] = slope * (place + (me * keys - keys * (count + 1)).astype(jnp.float32))
    dead = jnp.where(spot < lengths[...].reshape(1, 1), 0.0, DEAD)
    bias[heads:] = slope * (place - float(keys)) + dead
    mark = jnp.where(ids[...] == me, 1.0, 0.0)
    for shift in range(count):
        at = column(mark, rows, jnp.bitwise_xor(me, shift) * rows)
        mine[shift * rows : (shift + 1) * rows, :] = jnp.broadcast_to(at, (rows, LANES))


def tables(slopes, lengths, ids, rows, keys, after, brought):
    return pl.pallas_call(
        functools.partial(tables_kernel, rows),
        out_shape=(
            jax.ShapeDtypeStruct((2 * slopes.shape[0], keys), jnp.float32),
            jax.ShapeDtypeStruct((ids.shape[0], LANES), jnp.float32),
        ),
        in_specs=[VMEM] * 3 + [ANY, VMEM],
        out_specs=[VMEM] * 2,
        compiler_params=pltpu.CompilerParams(vmem_limit_bytes=8 << 20),
        name="tables",
    )(slopes, lengths, ids, after, brought)


def period(rows):
    return LANES // (rows // SUBLANES)


def attend_kernel(shifts, skipped, *refs):
    blocks, caches = refs[: len(shifts)], refs[len(shifts) : len(shifts) + 6]
    root_kt, root_v, branch_kt, branch_v, bias, mine = caches
    outs = refs[len(shifts) + 6 + skipped :]
    rows, width = blocks[0].shape
    heads = bias.shape[0] // 2
    size = width // heads
    every = rows * len(shifts)
    factor = LOG2E / math.sqrt(size)
    own = jnp.concatenate([mine[shift * rows : (shift + 1) * rows, :1] for shift in shifts] * 2, axis=0) > 0.5
    units = [(head, part) for head in range(0, heads, 2) for part in (0, 1)]

    def scores(unit):
        head, part = unit
        both = []
        for k in (head, head + 1):
            cols = slice(k * size, (k + 1) * size)
            query = jnp.concatenate([b[:, cols] for b in blocks], axis=0)
            key = (root_kt, branch_kt)[part][cols, :]
            both.append(jnp.dot(query, key, preferred_element_type=jnp.float32))
        return jnp.concatenate(both, axis=0)

    ahead = scores(units[0])
    lane = lax.broadcasted_iota(jnp.int32, (every, LANES), 1)
    place = lax.rem(lane, period(rows))
    level = jnp.zeros((every, LANES), jnp.float32)
    seen = []
    for i, (head, part) in enumerate(units):
        raw = ahead
        if i + 1 < len(units):
            ahead = scores(units[i + 1])
        shaped = []
        for k in range(2):
            row = part * heads + head + k
            shaped.append(raw[k * every : (k + 1) * every] * factor + bias[row : row + 1, :])
        shaped = jnp.concatenate(shaped, axis=0)
        top = jnp.max(shaped, axis=1, keepdims=True)
        weight = jnp.exp2(shaped - top)
        total = jnp.sum(weight, axis=1, keepdims=True)
        value = (root_v, branch_v)[part][:, head * size : (head + 2) * size]
        mixed = jnp.dot(weight.astype(value.dtype), value, preferred_element_type=jnp.float32)
        mixed = jnp.concatenate([mixed[:every, :size], mixed[every:, size:]], axis=0)
        seen.append((top, total, mixed))
        if part == 1:
            (top_r, total_r, mixed_r), (top_b, total_b, mixed_b) = seen
            seen = []
            top = jnp.maximum(top_r, jnp.where(own, top_b, DEAD))
            scale_r = jnp.exp2(top_r - top)
            scale_b = jnp.where(own, jnp.exp2(top_b - top), 0.0)
            total = scale_r * total_r + scale_b * total_b
            inverse = 1.0 / total
            mixed = (scale_r * inverse) * mixed_r + (scale_b * inverse) * mixed_b
            log = top + jnp.log2(total)
            for k in range(2):
                half = log[k * every : (k + 1) * every]
                level = jnp.where(lax.rem(place, heads) == head + k, half, level)
                for j, out in enumerate(outs):
                    at = slice(k * every + j * rows, k * every + (j + 1) * rows)
                    out[(head + k) * rows : (head + k + 1) * rows, :] = mixed[at].astype(out.dtype)
    high = level.astype(jnp.bfloat16).astype(jnp.float32)
    middle = (level - high).astype(jnp.bfloat16).astype(jnp.float32)
    low = level - high - middle
    coded = jnp.where(place < heads, high, jnp.where(place < 2 * heads, middle, low))
    coded = jnp.where(place < 3 * heads, coded, 0.0)
    group = lax.broadcasted_iota(jnp.int32, (SUBLANES, LANES), 1) // period(rows)
    for j, out in enumerate(outs):
        packed = jnp.zeros((SUBLANES, LANES), jnp.float32)
        for g in range(rows // SUBLANES):
            start = j * rows + g * SUBLANES
            packed = jnp.where(group == g, coded[start : start + SUBLANES], packed)
        packed = jnp.concatenate([packed, jnp.zeros_like(packed)], axis=0)
        out[heads * rows :, :] = packed.astype(out.dtype)


def attend(shifts, blocks, caches, after):
    rows, width = blocks[0].shape
    keys = caches[0].shape[1]
    heads = caches[4].shape[0] // 2
    return pl.pallas_call(
        functools.partial(attend_kernel, tuple(shifts), len(after)),
        out_shape=tuple(
            jax.ShapeDtypeStruct((heads * rows + 2 * SUBLANES, width // heads), jnp.bfloat16) for _ in shifts
        ),
        in_specs=[VMEM] * (len(blocks) + len(caches)) + [ANY] * len(after),
        out_specs=[VMEM] * len(shifts),
        compiler_params=pltpu.CompilerParams(vmem_limit_bytes=24 << 20),
        cost_estimate=pl.CostEstimate(
            flops=8 * rows * len(shifts) * width * keys,
            bytes_accessed=8 * keys * width,
            transcendentals=2 * rows * len(shifts) * keys * heads,
        ),
        name="attend",
    )(*blocks, *caches, *after)


def hold_kernel(*refs):
    pass


def hold(arrays, after=(), spent=4 << 20):
    return pl.pallas_call(
        hold_kernel,
        out_shape=tuple(jax.ShapeDtypeStruct(array.shape, array.dtype) for array in arrays),
        in_specs=[ANY] * (len(arrays) + len(after)),
        out_specs=[ANY] * len(arrays),
        input_output_aliases={i: i for i in range(len(arrays))},
        compiler_params=pltpu.CompilerParams(vmem_limit_bytes=1 << 20),
        cost_estimate=pl.CostEstimate(flops=0, bytes_accessed=spent, transcendentals=0),
        name="hold",
    )(*arrays, *after)


def spread_of(rows, heads, size):
    lane = lax.rem(lax.broadcasted_iota(jnp.int32, (LANES, heads * size), 0), period(rows))
    head = lax.broadcasted_iota(jnp.int32, (LANES, heads * size), 1) // size
    return jnp.where((lax.rem(lane, heads) == head) & (lane < 3 * heads), 1.0, 0.0).astype(jnp.bfloat16)


def opened(refs, rows, heads, spread):
    group = lax.broadcasted_iota(jnp.int32, (SUBLANES, LANES), 1) // period(rows)
    coded = []
    for ref in refs:
        packed = ref[heads * rows :, :].astype(jnp.float32)[:SUBLANES]
        coded += [jnp.where(group == g, packed, 0.0) for g in range(rows // SUBLANES)]
    coded = jnp.concatenate(coded, axis=0).astype(jnp.bfloat16)
    logs = jnp.dot(coded, spread, preferred_element_type=jnp.float32)
    values = [jnp.concatenate([ref[h * rows : (h + 1) * rows, :] for h in range(heads)], axis=1) for ref in refs]
    return [(value.astype(jnp.float32), logs[j * rows : (j + 1) * rows]) for j, value in enumerate(values)]


def gather_kernel(rows, heads, *refs):
    *messages, mixed, total, top, spread = refs
    spread[...] = spread_of(rows, heads, messages[0].shape[1])
    parts = opened(messages, rows, heads, spread[...])
    level = functools.reduce(jnp.maximum, [log for _, log in parts])
    scales = [jnp.exp2(log - level) for _, log in parts]
    top[...] = level
    total[...] = functools.reduce(jnp.add, scales)
    mixed[...] = functools.reduce(jnp.add, [scale * value for scale, (value, _) in zip(scales, parts)])


def gather(parts, rows, width):
    wide = jax.ShapeDtypeStruct((rows, width), jnp.float32)
    heads = width // parts[0].shape[1]
    return pl.pallas_call(
        functools.partial(gather_kernel, rows, heads),
        out_shape=(wide, wide, wide, jax.ShapeDtypeStruct((LANES, width), jnp.bfloat16)),
        in_specs=[VMEM] * len(parts),
        out_specs=(VMEM,) * 4,
        compiler_params=pltpu.CompilerParams(vmem_limit_bytes=8 << 20),
        cost_estimate=pl.CostEstimate(flops=0, bytes_accessed=1 << 20, transcendentals=0),
        name="gather",
    )(*parts)


def merge_kernel(mixed, total, top, spread, *refs):
    out = refs[-1]
    rows, width = out.shape
    parts = opened(refs[:-1], rows, width // refs[0].shape[1], spread[...])
    level = functools.reduce(jnp.maximum, [log for _, log in parts], top[...])
    scale = jnp.exp2(top[...] - level)
    whole, sums = scale * mixed[...], scale * total[...]
    for value, log in parts:
        scale = jnp.exp2(log - level)
        whole += scale * value
        sums += scale
    out[...] = (whole / sums).astype(out.dtype)


def merge(gathered, last, rows, width):
    return pl.pallas_call(
        merge_kernel,
        out_shape=jax.ShapeDtypeStruct((rows, width), jnp.bfloat16),
        in_specs=[VMEM] * (4 + len(last)),
        out_specs=VMEM,
        compiler_params=pltpu.CompilerParams(vmem_limit_bytes=8 << 20),
        name="merge",
    )(*gathered, *last)


def shards(queries, root_keys, root_values, branch_keys, branch_values, branch_lengths, branch_ids, slopes):
    count = lax.axis_size("seq")
    rows, width = queries.shape

    def swap(array, shift):
        return lax.ppermute(array, "seq", [(i, i ^ shift) for i in range(count)])

    near, across = (0, 1), tuple(range(2, count, 2))
    far = tuple(shift + 1 for shift in across) + across
    blocks = {shift: swap(queries, shift) for shift in across}
    blocks[0], blocks[1] = queries, swap(queries, 1)
    root_kt, branch_kt, root_v = load((root_keys, branch_keys), (root_values,), (), 46)
    arrived = hold([blocks[shift] for shift in across], (root_kt, blocks[1]))
    for shift, block in zip(across, arrived):
        blocks[shift], blocks[shift + 1] = block, swap(block, 1)
    bias, mine = tables(slopes, branch_lengths, branch_ids, rows, root_keys.shape[0], root_kt, branch_values)
    caches = (root_kt, root_v, branch_kt, branch_values, bias, mine)
    sent = attend(far, [blocks[s] for s in far], caches, ())
    got = [swap(array, shift) for array, shift in zip(sent, far)]
    kept, passed = attend(near, [blocks[s] for s in near], caches, sent[:1])
    gathered = gather([kept, *hold(got[1:])], rows, width)
    (last,) = hold(got[:1], gathered[:1])
    return merge(gathered, [last, swap(passed, 1)], rows, width)


def solution(mesh):
    in_specs = (
        P(("grp", "seq"), "head"),
        P(("grp", "seq"), "head"),
        P(("grp", "seq"), "head"),
        P(("grp", "seq"), "head"),
        P(("grp", "seq"), "head"),
        P(("grp", "seq")),
        P("grp"),
        P("head"),
    )
    out_specs = P(("grp", "seq"), "head")
    return jax.shard_map(shards, mesh=mesh, in_specs=in_specs, out_specs=out_specs, check_vma=False)
```

```python
import functools
import math

import jax
import jax.numpy as jnp
from jax import lax
from jax.experimental import pallas as pl
from jax.experimental.pallas import tpu as pltpu
from jax.sharding import PartitionSpec as P

LOG2E = math.log2(math.e)
DEAD = -1e30
LANES = 128
SUBLANES = 8
ANY = pl.BlockSpec(memory_space=pl.ANY)
HBM = pl.BlockSpec(memory_space=pltpu.HBM)
VMEM = pl.BlockSpec(memory_space=pltpu.VMEM)


def load_kernel(chunks, turned, straight, skipped, *refs):
    sources, outs = refs[: turned + straight], refs[turned + straight + skipped : 2 * (turned + straight) + skipped]
    sems = refs[-1]
    keys, width = sources[0].shape
    rows = keys // chunks
    copies = []
    for i in range(turned):
        for j in range(chunks):
            part = pl.ds(j * rows, rows)
            copies.append(
                pltpu.make_async_copy(sources[i].at[part], refs[-2].at[i, part], sems.at[i * chunks + j])
            )
    for i in range(turned, turned + straight):
        copies.append(pltpu.make_async_copy(sources[i], outs[i], sems.at[turned * chunks + i - turned]))
    for copy in copies[: turned * chunks]:
        copy.start()
    for i in range(turned):
        for j in range(chunks):
            copies[i * chunks + j].wait()
            if i == j == 0:
                for copy in copies[turned * chunks :]:
                    copy.start()
            part = slice(j * rows, (j + 1) * rows)
            for col in range(0, width, LANES):
                outs[i][col : col + LANES, part] = refs[-2][i, part, col : col + LANES].T
    for copy in copies[turned * chunks :]:
        copy.wait()


def load(turned, straight, after, limit):
    chunks = 2
    arrays = (*turned, *straight)
    keys, width = arrays[0].shape
    kind = arrays[0].dtype
    return pl.pallas_call(
        functools.partial(load_kernel, chunks, len(turned), len(straight), len(after)),
        out_shape=tuple(jax.ShapeDtypeStruct((width, keys), kind) for _ in turned)
        + tuple(jax.ShapeDtypeStruct((keys, width), kind) for _ in straight),
        in_specs=[HBM] * len(arrays) + [ANY] * len(after),
        out_specs=(VMEM,) * len(arrays),
        scratch_shapes=[pltpu.VMEM((len(turned), keys, width), kind)] * (len(turned) > 0)
        + [pltpu.SemaphoreType.DMA((len(turned) * chunks + len(straight),))],
        compiler_params=pltpu.CompilerParams(vmem_limit_bytes=limit << 20),
        cost_estimate=pl.CostEstimate(flops=0, bytes_accessed=2 * len(arrays) * keys * width, transcendentals=0),
        name="load",
    )(*arrays, *after)


def column(vector, rows, start):
    wide = jnp.broadcast_to(vector.reshape(1, -1), (rows, vector.shape[0]))
    lane = lax.broadcasted_iota(jnp.int32, wide.shape, 1)
    sub = lax.broadcasted_iota(jnp.int32, wide.shape, 0)
    return jnp.sum(jnp.where(lane == sub + start, wide, jnp.zeros_like(wide)), axis=1, keepdims=True)


def tables_kernel(rows, slopes, lengths, ids, after, brought, bias, mine):
    me = lax.axis_index("seq")
    count = lax.axis_size("seq")
    heads = slopes.shape[0]
    keys = bias.shape[1]
    slope = column(slopes[...], heads, 0) * LOG2E
    spot = lax.broadcasted_iota(jnp.int32, (1, keys), 1)
    place = spot.astype(jnp.float32)
    bias[:heads] = slope * (place + (me * keys - keys * (count + 1)).astype(jnp.float32))
    dead = jnp.where(spot < lengths[...].reshape(1, 1), 0.0, DEAD)
    bias[heads:] = slope * (place - float(keys)) + dead
    mark = jnp.where(ids[...] == me, 1.0, 0.0)
    for shift in range(count):
        at = column(mark, rows, jnp.bitwise_xor(me, shift) * rows)
        mine[shift * rows : (shift + 1) * rows, :] = jnp.broadcast_to(at, (rows, LANES))


def tables(slopes, lengths, ids, rows, keys, after, brought):
    return pl.pallas_call(
        functools.partial(tables_kernel, rows),
        out_shape=(
            jax.ShapeDtypeStruct((2 * slopes.shape[0], keys), jnp.float32),
            jax.ShapeDtypeStruct((ids.shape[0], LANES), jnp.float32),
        ),
        in_specs=[VMEM] * 3 + [ANY, VMEM],
        out_specs=[VMEM] * 2,
        compiler_params=pltpu.CompilerParams(vmem_limit_bytes=8 << 20),
        name="tables",
    )(slopes, lengths, ids, after, brought)


def period(rows):
    return LANES // (rows // SUBLANES)


def attend_kernel(shifts, skipped, *refs):
    blocks, caches = refs[: len(shifts)], refs[len(shifts) : len(shifts) + 6]
    root_kt, root_v, branch_kt, branch_v, bias, mine = caches
    outs = refs[len(shifts) + 6 + skipped :]
    rows, width = blocks[0].shape
    heads = bias.shape[0] // 2
    size = width // heads
    every = rows * len(shifts)
    factor = LOG2E / math.sqrt(size)
    own = jnp.concatenate([mine[shift * rows : (shift + 1) * rows, :1] for shift in shifts] * 2, axis=0) > 0.5
    units = [(head, part) for head in range(0, heads, 2) for part in (0, 1)]

    def scores(unit):
        head, part = unit
        both = []
        for k in (head, head + 1):
            cols = slice(k * size, (k + 1) * size)
            query = jnp.concatenate([b[:, cols] for b in blocks], axis=0)
            key = (root_kt, branch_kt)[part][cols, :]
            both.append(jnp.dot(query, key, preferred_element_type=jnp.float32))
        return jnp.concatenate(both, axis=0)

    ahead = scores(units[0])
    lane = lax.broadcasted_iota(jnp.int32, (every, LANES), 1)
    place = lax.rem(lane, period(rows))
    level = jnp.zeros((every, LANES), jnp.float32)
    seen = []
    for i, (head, part) in enumerate(units):
        raw = ahead
        if i + 1 < len(units):
            ahead = scores(units[i + 1])
        shaped = []
        for k in range(2):
            row = part * heads + head + k
            shaped.append(raw[k * every : (k + 1) * every] * factor + bias[row : row + 1, :])
        shaped = jnp.concatenate(shaped, axis=0)
        top = jnp.max(shaped, axis=1, keepdims=True)
        weight = jnp.exp2(shaped - top)
        total = jnp.sum(weight, axis=1, keepdims=True)
        value = (root_v, branch_v)[part][:, head * size : (head + 2) * size]
        mixed = jnp.dot(weight.astype(value.dtype), value, preferred_element_type=jnp.float32)
        mixed = jnp.concatenate([mixed[:every, :size], mixed[every:, size:]], axis=0)
        seen.append((top, total, mixed))
        if part == 1:
            (top_r, total_r, mixed_r), (top_b, total_b, mixed_b) = seen
            seen = []
            top = jnp.maximum(top_r, jnp.where(own, top_b, DEAD))
            scale_r = jnp.exp2(top_r - top)
            scale_b = jnp.where(own, jnp.exp2(top_b - top), 0.0)
            total = scale_r * total_r + scale_b * total_b
            inverse = 1.0 / total
            mixed = (scale_r * inverse) * mixed_r + (scale_b * inverse) * mixed_b
            log = top + jnp.log2(total)
            for k in range(2):
                half = log[k * every : (k + 1) * every]
                level = jnp.where(lax.rem(place, heads) == head + k, half, level)
                for j, out in enumerate(outs):
                    at = slice(k * every + j * rows, k * every + (j + 1) * rows)
                    out[(head + k) * rows : (head + k + 1) * rows, :] = mixed[at].astype(out.dtype)
    high = level.astype(jnp.bfloat16).astype(jnp.float32)
    middle = (level - high).astype(jnp.bfloat16).astype(jnp.float32)
    low = level - high - middle
    coded = jnp.where(place < heads, high, jnp.where(place < 2 * heads, middle, low))
    coded = jnp.where(place < 3 * heads, coded, 0.0)
    group = lax.broadcasted_iota(jnp.int32, (SUBLANES, LANES), 1) // period(rows)
    for j, out in enumerate(outs):
        packed = jnp.zeros((SUBLANES, LANES), jnp.float32)
        for g in range(rows // SUBLANES):
            start = j * rows + g * SUBLANES
            packed = jnp.where(group == g, coded[start : start + SUBLANES], packed)
        packed = jnp.concatenate([packed, jnp.zeros_like(packed)], axis=0)
        out[heads * rows :, :] = packed.astype(out.dtype)


def attend(shifts, blocks, caches, after):
    rows, width = blocks[0].shape
    keys = caches[0].shape[1]
    heads = caches[4].shape[0] // 2
    return pl.pallas_call(
        functools.partial(attend_kernel, tuple(shifts), len(after)),
        out_shape=tuple(
            jax.ShapeDtypeStruct((heads * rows + 2 * SUBLANES, width // heads), jnp.bfloat16) for _ in shifts
        ),
        in_specs=[VMEM] * (len(blocks) + len(caches)) + [ANY] * len(after),
        out_specs=[VMEM] * len(shifts),
        compiler_params=pltpu.CompilerParams(vmem_limit_bytes=24 << 20),
        cost_estimate=pl.CostEstimate(
            flops=8 * rows * len(shifts) * width * keys,
            bytes_accessed=8 * keys * width,
            transcendentals=2 * rows * len(shifts) * keys * heads,
        ),
        name="attend",
    )(*blocks, *caches, *after)


def hold_kernel(*refs):
    pass


def hold(arrays, after=(), spent=4 << 20):
    return pl.pallas_call(
        hold_kernel,
        out_shape=tuple(jax.ShapeDtypeStruct(array.shape, array.dtype) for array in arrays),
        in_specs=[ANY] * (len(arrays) + len(after)),
        out_specs=[ANY] * len(arrays),
        input_output_aliases={i: i for i in range(len(arrays))},
        compiler_params=pltpu.CompilerParams(vmem_limit_bytes=1 << 20),
        cost_estimate=pl.CostEstimate(flops=0, bytes_accessed=spent, transcendentals=0),
        name="hold",
    )(*arrays, *after)


def spread_of(rows, heads, size):
    lane = lax.rem(lax.broadcasted_iota(jnp.int32, (LANES, heads * size), 0), period(rows))
    head = lax.broadcasted_iota(jnp.int32, (LANES, heads * size), 1) // size
    return jnp.where((lax.rem(lane, heads) == head) & (lane < 3 * heads), 1.0, 0.0).astype(jnp.bfloat16)


def opened(refs, rows, heads, spread):
    group = lax.broadcasted_iota(jnp.int32, (SUBLANES, LANES), 1) // period(rows)
    coded = []
    for ref in refs:
        packed = ref[heads * rows :, :].astype(jnp.float32)[:SUBLANES]
        coded += [jnp.where(group == g, packed, 0.0) for g in range(rows // SUBLANES)]
    coded = jnp.concatenate(coded, axis=0).astype(jnp.bfloat16)
    logs = jnp.dot(coded, spread, preferred_element_type=jnp.float32)
    values = [jnp.concatenate([ref[h * rows : (h + 1) * rows, :] for h in range(heads)], axis=1) for ref in refs]
    return [(value.astype(jnp.float32), logs[j * rows : (j + 1) * rows]) for j, value in enumerate(values)]


def gather_kernel(rows, heads, *refs):
    *messages, mixed, total, top, spread = refs
    spread[...] = spread_of(rows, heads, messages[0].shape[1])
    parts = opened(messages, rows, heads, spread[...])
    level = functools.reduce(jnp.maximum, [log for _, log in parts])
    scales = [jnp.exp2(log - level) for _, log in parts]
    top[...] = level
    total[...] = functools.reduce(jnp.add, scales)
    mixed[...] = functools.reduce(jnp.add, [scale * value for scale, (value, _) in zip(scales, parts)])


def gather(parts, rows, width):
    wide = jax.ShapeDtypeStruct((rows, width), jnp.float32)
    heads = width // parts[0].shape[1]
    return pl.pallas_call(
        functools.partial(gather_kernel, rows, heads),
        out_shape=(wide, wide, wide, jax.ShapeDtypeStruct((LANES, width), jnp.bfloat16)),
        in_specs=[VMEM] * len(parts),
        out_specs=(VMEM,) * 4,
        compiler_params=pltpu.CompilerParams(vmem_limit_bytes=8 << 20),
        cost_estimate=pl.CostEstimate(flops=0, bytes_accessed=1 << 20, transcendentals=0),
        name="gather",
    )(*parts)


def merge_kernel(mixed, total, top, spread, *refs):
    out = refs[-1]
    rows, width = out.shape
    parts = opened(refs[:-1], rows, width // refs[0].shape[1], spread[...])
    level = functools.reduce(jnp.maximum, [log for _, log in parts], top[...])
    scale = jnp.exp2(top[...] - level)
    whole, sums = scale * mixed[...], scale * total[...]
    for value, log in parts:
        scale = jnp.exp2(log - level)
        whole += scale * value
        sums += scale
    out[...] = (whole / sums).astype(out.dtype)


def merge(gathered, last, rows, width):
    return pl.pallas_call(
        merge_kernel,
        out_shape=jax.ShapeDtypeStruct((rows, width), jnp.bfloat16),
        in_specs=[VMEM] * (4 + len(last)),
        out_specs=VMEM,
        compiler_params=pltpu.CompilerParams(vmem_limit_bytes=8 << 20),
        name="merge",
    )(*gathered, *last)


def shards(queries, root_keys, root_values, branch_keys, branch_values, branch_lengths, branch_ids, slopes):
    count = lax.axis_size("seq")
    rows, width = queries.shape

    def swap(array, shift):
        return lax.ppermute(array, "seq", [(i, i ^ shift) for i in range(count)])

    near, across = (0, 1), tuple(range(2, count, 2))
    far = tuple(shift + 1 for shift in across) + across
    blocks = {shift: swap(queries, shift) for shift in across}
    blocks[0], blocks[1] = queries, swap(queries, 1)
    root_kt, branch_kt, root_v = load((root_keys, branch_keys), (root_values,), (), 46)
    arrived = hold([blocks[shift] for shift in across], (root_kt, blocks[1]))
    for shift, block in zip(across, arrived):
        blocks[shift], blocks[shift + 1] = block, swap(block, 1)
    bias, mine = tables(slopes, branch_lengths, branch_ids, rows, root_keys.shape[0], root_kt, branch_values)
    caches = (root_kt, root_v, branch_kt, branch_values, bias, mine)
    sent = attend(far, [blocks[s] for s in far], caches, ())
    got = [swap(array, shift) for array, shift in zip(sent, far)]
    kept, passed = attend(near, [blocks[s] for s in near], caches, sent[:1])
    gathered = gather([kept, *hold(got[1:])], rows, width)
    (last,) = hold(got[:1], gathered[:1])
    return merge(gathered, [last, swap(passed, 1)], rows, width)


def solution(mesh):
    in_specs = (
        P(("grp", "seq"), "head"),
        P(("grp", "seq"), "head"),
        P(("grp", "seq"), "head"),
        P(("grp", "seq"), "head"),
        P(("grp", "seq"), "head"),
        P(("grp", "seq")),
        P("grp"),
        P("head"),
    )
    out_specs = P(("grp", "seq"), "head")
    return jax.shard_map(shards, mesh=mesh, in_specs=in_specs, out_specs=out_specs, check_vma=False)
```
